128 devices in a mesh: group: 16 (over z, x), inner: 8 (over y, core).
Axes of the slice: x: 4, y: 4, z: 4, core: 2. Of those that a mesh axis runs over, the one named last changes fastest.
Arguments:
- density_matrix: bfloat16 [8192, 8192], P('group', 'inner'), may hold values from -0.0029296875 to 0.0029296875
- basis_values: bfloat16 [128, 1536, 2048], P(('group', 'inner')), may hold values from -6 to 6
- block_list: int32 [128, 16], P(('group', 'inner')), may hold values from 0 to 63, as said below
- point_counts: int32 [128], P(('group', 'inner')), may hold values from 1 to 1536, 122880 in all
- core_density: float32 [128, 1536], P(('group', 'inner')), may hold values from 0.5 to 4
- grid_weights: float32 [128, 1536], P(('group', 'inner')), may hold values from 0.0001 to 0.002
Outputs:
- density: float32 [128, 1536], P(('group', 'inner'))
- xc_matrix: float32 [8192, 8192], P('group', 'inner')
The draws below stay inside these ranges and needn't reach their ends.
Inputs may be any that keep to these rules, and one draw needn't show every extreme that they name: `block_list`: entry i of every batch's list lies in blocks i * 4 to (i + 1) * 4 - 1.
All inputs are finite; a program needn't handle non-finite values. No bound on the sum of `point_counts` on one device may be relied on, other than what follows from the above.
Results may differ from the reference program's by a relative error of at most 0.00095.
Values may be sent and summed in bfloat16 or wider, within the bound.
No kernel may reach another device: no remote copies, remote signals or barrier semaphores. Data moves between devices by JAX's collectives and lax.ppermute only.
A program may use at most 128 MiB of HBM per device.

```python
import math
import jax
import jax.numpy as jnp
import numpy as np
from jax import lax

NBF = 8192
BLK = 128
KB = 16
PTS = 1536
SPAN = 4
NBAT = 128


def draw_block_list(key, part):
    offsets = jax.random.randint(key, (NBAT, KB), 0, SPAN, dtype=jnp.int32)
    return (offsets + jnp.arange(KB, dtype=jnp.int32)[None, :] * SPAN).astype(jnp.int32)


def steps_of(own_key, dims, pieces, low, high):
    factor_of = 1.0
    for axis_at, shards_of in pieces:
        heights = jax.random.uniform(jax.random.fold_in(jax.random.fold_in(own_key, 6), axis_at), (shards_of,), jnp.float32, low / len(pieces), high / len(pieces))
        factor_of = factor_of * jnp.repeat(jnp.exp(heights), dims[axis_at] // shards_of).reshape((-1,) + (1,) * (len(dims) - 1 - axis_at))
    return factor_of


def length_profile(number_of, total, most, skew):
    loads = [(1 << 20) // math.isqrt(standing ** skew) + 1 for standing in range(2, number_of + 1)]
    surplus, counts = total - most - (number_of - 1), [1] * (number_of - 1)
    while surplus > 0:
        free = [i for i in range(number_of - 1) if counts[i] < most]
        whole, budget = sum([loads[i] for i in free]), surplus
        for i in free:
            more = min(most - counts[i], max(1, budget * loads[i] // whole), surplus)
            counts[i] = counts[i] + more
            surplus = surplus - more
    return np.array([most] + counts)


def ragged_sizes(key, amount, total, most, slope):
    if amount == 2:
        one = jax.random.randint(key, (), max(1, total - most), min(most, total - 1) + 1)
        return jnp.stack([one, total - one])
    tallies = jnp.asarray(length_profile(amount, total, most, slope), jnp.int32)
    twos = (amount - 1) // 2
    source_of, sink = tallies[1:1 + 2 * twos:2], tallies[2:2 + 2 * twos:2]
    slack = jnp.minimum(source_of - 1, most - sink)
    moved = jax.random.randint(jax.random.fold_in(key, 1), (twos,), 0, 1 << 20) % (slack + 1)
    tallies = tallies.at[1:1 + 2 * twos:2].set(source_of - moved).at[2:2 + 2 * twos:2].set(sink + moved)
    return tallies[jax.random.permutation(jax.random.fold_in(key, 2), amount)]


def centred(rng, dims, deviation, limit, pieces=(), kind=jnp.bfloat16):
    gain = steps_of(rng, dims, pieces, -0.22, 0.18) if pieces else 1.0
    entries = jax.random.normal(rng, dims, jnp.float32) * deviation * gain
    return jnp.minimum(jnp.maximum(entries, -limit), limit).astype(kind)


def setup_inputs(seed: int = 0) -> dict:
    keys = jax.random.split(jax.random.key(seed), 7)
    density_matrix = centred(keys[0], (NBF, NBF), ((KB * BLK) ** 2) ** -0.5, 0.0029296875, ((0, 16), (1, 8)))
    basis_values = centred(keys[1], (NBAT, PTS, KB * BLK), 1.0, 6.0, ((0, 128),))
    block_list = draw_block_list(jax.random.fold_in(keys[6], 71), 0)
    point_counts = ragged_sizes(keys[3], NBAT, NBAT * PTS * 5 // 8, PTS, 2).astype(jnp.int32)
    core_density = jnp.clip(jnp.exp(math.log(4.0) - 2.0794415 * jax.random.uniform(keys[4], (NBAT, PTS), jnp.float32) ** steps_of(keys[4], (NBAT, PTS), ((0, 128),), -0.2, 0.2)), 0.5, 4.0)
    grid_weights = jnp.clip(jnp.exp(math.log(0.002) - 2.9957323 * jax.random.uniform(keys[5], (NBAT, PTS), jnp.float32) ** steps_of(keys[5], (NBAT, PTS), ((0, 128),), -0.2, 0.2)), 0.0001, 0.002)
    return {"density_matrix": density_matrix, "basis_values": basis_values, "block_list": block_list, "point_counts": point_counts, "core_density": core_density, "grid_weights": grid_weights}


slater_factor = -(3.0 / 3.141592653589793) ** (1.0 / 3.0)
density_floor = 0.1


def one_batch(basis_table, listed, core_values, weights, live_count, density_matrix):
    row_index = (listed[:, None] * BLK + jnp.arange(BLK, dtype=jnp.int32)[None, :]).reshape(-1).astype(jnp.int32)
    sub_matrix = jnp.take(jnp.take(density_matrix, row_index, axis=0), row_index, axis=1)
    projected = jnp.dot(basis_table, sub_matrix, preferred_element_type=jnp.float32)
    density = core_values + jnp.sum(projected * basis_table.astype(jnp.float32), axis=1)
    potential = slater_factor * jnp.cbrt(jnp.maximum(density, density_floor))
    live_mask = jnp.arange(PTS, dtype=jnp.int32) < live_count
    integrand = jnp.where(live_mask, weights * potential, jnp.zeros_like(potential))
    weighted = (integrand[:, None] * basis_table).astype(jnp.bfloat16)
    partial_value = jnp.dot(basis_table.T, weighted, preferred_element_type=jnp.float32)
    return row_index, density, partial_value


def reference(density_matrix, basis_values, block_list, point_counts, core_density, grid_weights):
    def batch_step(accumulated, inputs):
        basis_table, listed, core_values, weights, live_count = inputs
        row_index, density, partial_value = one_batch(basis_table, listed, core_values, weights, live_count, density_matrix)
        accumulated = accumulated.at[row_index[:, None], row_index[None, :]].add(partial_value)
        return accumulated, density

    initial = jnp.zeros((NBF, NBF), jnp.float32)
    accumulated, density = lax.scan(batch_step, initial, (basis_values, block_list, core_density, grid_weights, point_counts))
    return density, accumulated
```

```python
import jax
import jax.numpy as jnp
from jax import lax
from jax.experimental import pallas as pl
from jax.experimental.pallas import tpu as pltpu
from jax.sharding import PartitionSpec as P

BLK = 128
KB = 16
GROUPS = 16
INNERS = 8
DEVICES = GROUPS * INNERS
SPAN = 4
SLOT = SPAN * BLK
BUCKETS = SPAN * SPAN
ROWS = BLK + 8
PTS = 1536
COLS = KB * BLK
PAIR = 2 * BLK
AXES = ("group", "inner")

slater_factor = -((3.0 / 3.141592653589793) ** (1.0 / 3.0))
density_floor = 0.1
STEP = float(2**22)
BITS = 14.0
TINY = 2.0**-100
TILE = 512
VMEM_BATCH = 44 * 2**20


def owner(i, j):
    return i * INNERS + j // 2 if (i + j) % 2 == 0 else j * INNERS + i // 2


def chosen_half(g, n):
    odd = g % 2
    return odd if g < 2 * n else 1 - odd


def mirror_pairs():
    pairs = []
    for g in range(GROUPS):
        for n in range(INNERS):
            half = chosen_half(g, n)
            if g // 2 != n:
                half = 1 - half
            pairs.append((g * INNERS + n, (2 * n + half) * INNERS + g // 2))
    return pairs


def row_col(shape):
    return lax.broadcasted_iota(jnp.int32, shape, 0), lax.broadcasted_iota(jnp.int32, shape, 1)


def encode(value):
    return jnp.floor(value * STEP + 0.5).astype(jnp.int32).astype(jnp.int16)


def pick_kernel(flags, index, own, other, mirror, out, table):
    step = pl.program_id(0)
    per_step = out.shape[0]

    @pl.when(step == 0)
    def _():
        flip = flags[0] == 1
        special = flags[1] == 1
        low = flags[2] == 1

        def put(a, b, first, second):
            rows, cols = row_col((BLK, BLK))
            total = first + second.T
            diagonal = jnp.sum(jnp.where(rows == cols, total, 0.0), axis=0, keepdims=True)
            tail = jnp.broadcast_to(diagonal, (ROWS - BLK, BLK))
            table[a * SPAN + b] = encode(jnp.concatenate([total, tail], axis=0))

            @pl.when(special)
            def _():
                at = jnp.where(low, a, b)
                start = pl.multiple_of(at * BLK, BLK)
                block = other[pl.ds(start, BLK), pl.ds(start, BLK)].astype(jnp.float32)
                both = jnp.where(rows == cols, block, block + block.T)
                keep = jnp.where(low, rows - cols, cols - rows) > 0
                packed = jnp.where(keep, total, both)
                table[a * SPAN + b] = encode(jnp.concatenate([packed, tail], axis=0))

        def block_of(ref, a, b):
            return ref[a * BLK : (a + 1) * BLK, b * BLK : (b + 1) * BLK].astype(jnp.float32)

        for a in range(SPAN):
            for b in range(SPAN):

                @pl.when(flip)
                def _():
                    put(a, b, block_of(mirror, a, b), block_of(own, b, a))

                @pl.when(jnp.logical_not(flip))
                def _():
                    put(a, b, block_of(own, a, b), block_of(mirror, b, a))

    def copy(k, carry):
        out[k] = table[index[step * per_step + k]]
        return carry

    lax.fori_loop(0, per_step, copy, 0, unroll=4)


def pick(flags, index, own, other, mirror):
    per_step = 16
    whole = pl.BlockSpec((SLOT, SLOT), lambda s: (0, 0))
    return pl.pallas_call(
        pick_kernel,
        grid=(DEVICES // per_step,),
        out_shape=jax.ShapeDtypeStruct((DEVICES, ROWS, BLK), jnp.int16),
        in_specs=[
            pl.BlockSpec(memory_space=pltpu.SMEM),
            pl.BlockSpec(memory_space=pltpu.SMEM),
            whole,
            whole,
            whole,
        ],
        out_specs=pl.BlockSpec((per_step, ROWS, BLK), lambda s: (s, 0, 0)),
        scratch_shapes=[pltpu.VMEM((BUCKETS, ROWS, BLK), jnp.int16)],
        compiler_params=pltpu.CompilerParams(vmem_limit_bytes=24 * 2**20),
    )(flags, index, own, other, mirror)


def pack(value):
    most = jnp.max(jnp.abs(value), axis=0, keepdims=True)
    power = jnp.ceil(jnp.log2(jnp.maximum(most, TINY)))
    scaled = jnp.floor(value * jnp.exp2(BITS - power) + 0.5).astype(jnp.int32)
    rows, _ = row_col(value.shape)
    return jnp.where(rows > BLK, power.astype(jnp.int32), scaled).astype(jnp.int16)


def unpack(coded):
    wide = coded.astype(jnp.int32).astype(jnp.float32)
    return wide * jnp.exp2(wide[BLK + 1 : BLK + 2] - BITS)


def batch_kernel(
    count,
    blocks_in,
    basis_in,
    turned_in,
    core,
    weights,
    density,
    pieces_out,
    blocks,
    basis,
    turned,
    pieces,
    both,
    total,
    scaled,
    arrived,
    left_here,
):
    loads = [
        pltpu.make_async_copy(source, target, arrived.at[k])
        for k, (source, target) in enumerate(
            ((blocks_in, blocks), (basis_in, basis), (turned_in, turned))
        )
    ]
    for load in loads:
        load.start()

    rows, cols = row_col((BLK, BLK))

    def message(device):
        return blocks[device].astype(jnp.int32).astype(jnp.float32)

    def place(i, j, value):
        top = value.astype(jnp.bfloat16)
        side = j % 2 * BLK
        at = slice(i * BLK, (i + 1) * BLK)
        half = j // 2 % 2
        both[half, at, side : side + BLK] = top
        both[half, at, PAIR + side : PAIR + side + BLK] = (value - top.astype(jnp.float32)).astype(jnp.bfloat16)

    loads[0].wait()
    for big in range(KB // 2):
        for i in range(2 * big):
            for j in (2 * big, 2 * big + 1):
                place(i, j, message(owner(i, j))[:BLK])
        i = 2 * big
        first = message(i * INNERS + big)
        second = message((i + 1) * INNERS + big)
        diagonal = jnp.broadcast_to(first[BLK : BLK + 1], (BLK, BLK))
        first, second = first[:BLK], second[:BLK]
        place(i, i, jnp.where(rows <= cols, first, 0.0))
        place(i + 1, i + 1, jnp.where(rows >= cols, second, 0.0))
        place(i, i + 1, jnp.where(rows > cols, first, jnp.where(rows < cols, second, diagonal)))
        place(i + 1, i, jnp.zeros((BLK, BLK), jnp.float32))
        depth = (big + 1) * PAIR
        if big == 0:
            loads[1].wait()
        for m in range(PTS // TILE):
            at = slice(m * TILE, (m + 1) * TILE)
            product = jnp.dot(
                basis[at, :depth], both[big % 2, :depth], preferred_element_type=jnp.float32
            )
            product = product[:, :PAIR] + product[:, PAIR:]
            product *= basis[at, big * PAIR : (big + 1) * PAIR].astype(jnp.float32)
            folded = product[:, :BLK] + product[:, BLK:]
            total[at] = folded if big == 0 else total[at] + folded

    summed = jnp.sum(total[...], axis=1, keepdims=True) * (1.0 / STEP)
    found = core[...] + summed
    density[...] = found
    potential = slater_factor * jnp.exp(jnp.log(jnp.maximum(found, density_floor)) * (1.0 / 3.0))
    live = lax.broadcasted_iota(jnp.int32, (PTS, 1), 0) < count[0]
    integrand = jnp.where(live, weights[...] * potential, 0.0)

    tail = jnp.zeros((ROWS - BLK, BLK), jnp.float32)

    def send(device, value, last=tail):
        pieces[device] = pack(jnp.concatenate([value, last], axis=0))
        pltpu.make_async_copy(pieces.at[device], pieces_out.at[device], left_here).start()

    loads[2].wait()
    for big in range(KB // 2):
        lanes = slice(big * PAIR, (big + 1) * PAIR)
        half = big % 2
        scaled[half] = (integrand * basis[:, lanes].astype(jnp.float32)).astype(jnp.bfloat16)
        products = jnp.dot(
            turned[: (big + 1) * PAIR], scaled[half], preferred_element_type=jnp.float32
        )
        for part in range(big + 1):
            product = products[part * PAIR : (part + 1) * PAIR]
            i, j = 2 * part, 2 * big
            if part < big:
                for di in range(2):
                    for dj in range(2):
                        send(
                            owner(i + di, j + dj),
                            product[di * BLK : (di + 1) * BLK, dj * BLK : (dj + 1) * BLK],
                        )
            else:
                cross = product[:BLK, BLK:]
                diagonal = jnp.sum(jnp.where(rows == cols, cross, 0.0), axis=0, keepdims=True)
                last = jnp.broadcast_to(diagonal, (ROWS - BLK, BLK))
                send(i * INNERS + big, jnp.where(rows > cols, cross, product[:BLK, :BLK]), last)
                send((i + 1) * INNERS + big, jnp.where(rows < cols, cross, product[BLK:, BLK:]), last)
    pltpu.make_async_copy(pieces, pieces_out, left_here).wait()


def batch(count, blocks, basis, turned, core, weights):
    vmem = pl.BlockSpec(memory_space=pltpu.VMEM)
    anywhere = pl.BlockSpec(memory_space=pl.ANY)
    messages = (DEVICES, ROWS, BLK)
    return pl.pallas_call(
        batch_kernel,
        out_shape=(
            jax.ShapeDtypeStruct((PTS, 1), jnp.float32),
            jax.ShapeDtypeStruct(messages, jnp.int16),
        ),
        in_specs=[pl.BlockSpec(memory_space=pltpu.SMEM)] + [anywhere] * 3 + [vmem] * 2,
        out_specs=(vmem, pl.BlockSpec(memory_space=pltpu.HBM)),
        scratch_shapes=[
            pltpu.VMEM(messages, jnp.int16),
            pltpu.VMEM((PTS, COLS), jnp.bfloat16),
            pltpu.VMEM((COLS, PTS), jnp.bfloat16),
            pltpu.VMEM(messages, jnp.int16),
            pltpu.VMEM((2, COLS, 2 * PAIR), jnp.bfloat16),
            pltpu.VMEM((PTS, BLK), jnp.float32),
            pltpu.VMEM((2, PTS, PAIR), jnp.bfloat16),
            pltpu.SemaphoreType.DMA((3,)),
            pltpu.SemaphoreType.DMA,
        ],
        compiler_params=pltpu.CompilerParams(vmem_limit_bytes=VMEM_BATCH),
    )(count, blocks, basis, turned, core, weights)


def sum_kernel(index, pieces, total, copy):
    step = pl.program_id(0)
    per_step = pieces.shape[0]

    @pl.when(step == 0)
    def _():
        total[...] = jnp.zeros_like(total)

    def add(k, carry):
        at = index[step * per_step + k]
        total[at] = total[at] + unpack(pieces[k])
        return carry

    lax.fori_loop(0, per_step, add, 0, unroll=4)

    @pl.when(step == pl.num_programs(0) - 1)
    def _():
        for k in range(BUCKETS):
            copy[k] = pack(total[k])


def sum_pieces(index, pieces):
    per_step = 16
    shape = (BUCKETS, ROWS, BLK)
    whole = pl.BlockSpec(shape, lambda s: (0, 0, 0))
    return pl.pallas_call(
        sum_kernel,
        grid=(DEVICES // per_step,),
        out_shape=(jax.ShapeDtypeStruct(shape, jnp.float32), jax.ShapeDtypeStruct(shape, jnp.int16)),
        in_specs=[
            pl.BlockSpec(memory_space=pltpu.SMEM),
            pl.BlockSpec((per_step, ROWS, BLK), lambda s: (s, 0, 0)),
        ],
        out_specs=(whole, whole),
        compiler_params=pltpu.CompilerParams(vmem_limit_bytes=24 * 2**20),
    )(index, pieces)


def finish_kernel(flags, total, mirror, out):
    flip = flags[0] == 1
    special = flags[1] == 1
    half = flags[3]
    rows, cols = row_col((BLK, BLK))

    def slot(which, a, b):
        start = pl.multiple_of(which * SLOT + b * BLK, BLK)
        return (slice(a * BLK, (a + 1) * BLK), pl.ds(start, BLK))

    def received(k):
        return unpack(mirror[k])

    @pl.when(jnp.logical_not(special))
    def _():
        for a in range(SPAN):
            for b in range(SPAN):
                k = a * SPAN + b

                @pl.when(flip)
                def _():
                    out[slot(half, b, a)] = total[k, :BLK].T
                    out[slot(1 - half, b, a)] = received(k)[:BLK].T

                @pl.when(jnp.logical_not(flip))
                def _():
                    out[slot(half, a, b)] = total[k, :BLK]
                    out[slot(1 - half, a, b)] = received(k)[:BLK]

    def diagonal_group(lower):
        for a in range(SPAN):
            for b in range(SPAN):
                k = a * SPAN + b
                mine, theirs = total[k], received(k)
                first, second = (mine, theirs) if lower else (theirs, mine)
                middle = jnp.broadcast_to(first[BLK : BLK + 1], (BLK, BLK))
                cross = jnp.where(
                    rows > cols, first[:BLK], jnp.where(rows < cols, second[:BLK], middle)
                )
                if lower:
                    out[slot(half, a, b)] = cross
                else:
                    out[slot(half, b, a)] = cross.T
                if a != b:
                    out[slot(1 - half, a, b)] = jnp.zeros((BLK, BLK), jnp.float32)
        for a in range(SPAN):
            held = jnp.zeros((BLK, BLK), jnp.float32)
            for b in range(SPAN):
                held += total[a * SPAN + b if lower else b * SPAN + a, :BLK]
            keep = rows < cols if lower else rows > cols
            strict = jnp.where(keep, held, 0.0)
            out[slot(1 - half, a, a)] = jnp.where(rows == cols, held, strict + strict.T)

    @pl.when(jnp.logical_and(special, flags[2] == 1))
    def _():
        diagonal_group(True)

    @pl.when(jnp.logical_and(special, flags[2] == 0))
    def _():
        diagonal_group(False)


def finish(flags, total, mirror):
    vmem = pl.BlockSpec(memory_space=pltpu.VMEM)
    return pl.pallas_call(
        finish_kernel,
        out_shape=jax.ShapeDtypeStruct((SLOT, 2 * SLOT), jnp.float32),
        in_specs=[pl.BlockSpec(memory_space=pltpu.SMEM), vmem, vmem],
        out_specs=vmem,
        compiler_params=pltpu.CompilerParams(vmem_limit_bytes=24 * 2**20),
    )(flags, total, mirror)


def per_device(density_matrix, basis_values, block_list, point_counts, core_density, grid_weights):
    g = lax.axis_index("group")
    n = lax.axis_index("inner")
    odd = lax.rem(g, 2)
    half = jnp.where(g < 2 * n, odd, 1 - odd)
    flip = (g > 2 * n).astype(jnp.int32)
    special = g // 2 == n
    column_slot = 2 * n + half
    first, second = jnp.minimum(g, column_slot), jnp.maximum(g, column_slot)
    flags = jnp.stack([flip, special.astype(jnp.int32), 1 - odd, half]).astype(jnp.int32)
    pairs = mirror_pairs()

    basis = basis_values[0]
    lists = lax.all_to_all(
        jnp.broadcast_to(block_list, (DEVICES, KB)), AXES, split_axis=0, concat_axis=0, tiled=True
    )
    left, right = density_matrix[:, :SLOT], density_matrix[:, SLOT:]
    own = jnp.where(half == 0, left, right)
    other = jnp.where(half == 0, right, left)
    mirror = lax.ppermute(jnp.where(special, own, other), AXES, pairs)
    slots = jnp.arange(KB, dtype=jnp.int32)
    factor = jnp.where(slots == first, SPAN, 0) + jnp.where(slots == second, 1, 0)
    index = jnp.sum((lists - slots * SPAN) * factor, axis=1).astype(jnp.int32)

    picked = pick(flags, index, own, other, mirror)
    blocks = lax.all_to_all(picked, AXES, split_axis=0, concat_axis=0, tiled=True)
    density, pieces = batch(
        point_counts,
        blocks,
        basis,
        basis.T,
        core_density.reshape(PTS, 1),
        grid_weights.reshape(PTS, 1),
    )
    landed = lax.all_to_all(pieces, AXES, split_axis=0, concat_axis=0, tiled=True)
    total, copy = sum_pieces(index, landed)
    returned = lax.ppermute(copy, AXES, [(target, source) for source, target in pairs])
    return density.reshape(1, PTS), finish(flags, total, returned)


def solution(mesh):
    return jax.shard_map(
        per_device,
        mesh=mesh,
        in_specs=(
            P("group", "inner"),
            P(AXES, None, None),
            P(AXES, None),
            P(AXES),
            P(AXES, None),
            P(AXES, None),
        ),
        out_specs=(P(AXES, None), P("group", "inner")),
        check_vma=False,
    )
```

```python
import jax
import jax.numpy as jnp
from jax import lax
from jax.experimental import pallas as pl
from jax.experimental.pallas import tpu as pltpu
from jax.sharding import PartitionSpec as P

BLK = 128
KB = 16
GROUPS = 16
INNERS = 8
DEVICES = GROUPS * INNERS
SPAN = 4
SLOT = SPAN * BLK
BUCKETS = SPAN * SPAN
ROWS = BLK + 8
PTS = 1536
COLS = KB * BLK
PAIR = 2 * BLK
AXES = ("group", "inner")

slater_factor = -((3.0 / 3.141592653589793) ** (1.0 / 3.0))
density_floor = 0.1
STEP = float(2**22)
BITS = 14.0
TINY = 2.0**-100
TILE = 512
CHUNK = 512
VMEM_ALL = 60 * 2**20
VMEM_SMALL = 24 * 2**20


def owner(i, j):
    return i * INNERS + j // 2 if (i + j) % 2 == 0 else j * INNERS + i // 2


def chosen_half(g, n):
    odd = g % 2
    return odd if g < 2 * n else 1 - odd


def mirror_pairs():
    pairs = []
    for g in range(GROUPS):
        for n in range(INNERS):
            half = chosen_half(g, n)
            if g // 2 != n:
                half = 1 - half
            pairs.append((g * INNERS + n, (2 * n + half) * INNERS + g // 2))
    return pairs


def row_col(shape):
    return lax.broadcasted_iota(jnp.int32, shape, 0), lax.broadcasted_iota(jnp.int32, shape, 1)


def encode(value):
    return jnp.floor(value * STEP + 0.5).astype(jnp.int32).astype(jnp.int16)


def pick_kernel(flags, index, matrix, mirror, out, table):
    step = pl.program_id(0)
    per_step = out.shape[0]

    @pl.when(step == 0)
    def _():
        flip = flags[0] == 1
        special = flags[1] == 1
        low = flags[2] == 1
        own_start = flags[3] * SLOT
        other_start = SLOT - own_start

        def put(a, b, first, second):
            rows, cols = row_col((BLK, BLK))
            total = first + second.T
            diagonal = jnp.sum(jnp.where(rows == cols, total, 0.0), axis=0, keepdims=True)
            tail = jnp.broadcast_to(diagonal, (ROWS - BLK, BLK))
            table[a * SPAN + b] = encode(jnp.concatenate([total, tail], axis=0))

            @pl.when(special)
            def _():
                at = jnp.where(low, a, b)
                start = pl.multiple_of(at * BLK, BLK)
                side = pl.multiple_of(other_start + at * BLK, BLK)
                block = matrix[pl.ds(start, BLK), pl.ds(side, BLK)].astype(jnp.float32)
                both = jnp.where(rows == cols, block, block + block.T)
                keep = jnp.where(low, rows - cols, cols - rows) > 0
                packed = jnp.where(keep, total, both)
                table[a * SPAN + b] = encode(jnp.concatenate([packed, tail], axis=0))

        def mirror_block(a, b):
            return mirror[a * BLK : (a + 1) * BLK, b * BLK : (b + 1) * BLK].astype(jnp.float32)

        def own_block(a, b):
            start = pl.multiple_of(own_start + b * BLK, BLK)
            return matrix[a * BLK : (a + 1) * BLK, pl.ds(start, BLK)].astype(jnp.float32)

        for a in range(SPAN):
            for b in range(SPAN):

                @pl.when(flip)
                def _():
                    put(a, b, mirror_block(a, b), own_block(b, a))

                @pl.when(jnp.logical_not(flip))
                def _():
                    put(a, b, own_block(a, b), mirror_block(b, a))

    def copy(k, carry):
        out[k] = table[index[step * per_step + k]]
        return carry

    lax.fori_loop(0, per_step, copy, 0, unroll=4)


def pick(flags, index, matrix, mirror):
    per_step = 16
    return pl.pallas_call(
        pick_kernel,
        grid=(DEVICES // per_step,),
        out_shape=jax.ShapeDtypeStruct((DEVICES, ROWS, BLK), jnp.int16),
        in_specs=[
            pl.BlockSpec(memory_space=pltpu.SMEM),
            pl.BlockSpec(memory_space=pltpu.SMEM),
            pl.BlockSpec((SLOT, 2 * SLOT), lambda s: (0, 0)),
            pl.BlockSpec((SLOT, SLOT), lambda s: (0, 0)),
        ],
        out_specs=pl.BlockSpec((per_step, ROWS, BLK), lambda s: (s, 0, 0)),
        scratch_shapes=[pltpu.VMEM((BUCKETS, ROWS, BLK), jnp.int16)],
        compiler_params=pltpu.CompilerParams(vmem_limit_bytes=VMEM_SMALL),
    )(flags, index, matrix, mirror)


def pack(value):
    most = jnp.max(jnp.abs(value), axis=0, keepdims=True)
    power = jnp.ceil(jnp.log2(jnp.maximum(most, TINY)))
    scaled = jnp.floor(value * jnp.exp2(BITS - power) + 0.5).astype(jnp.int32)
    rows, _ = row_col(value.shape)
    return jnp.where(rows > BLK, power.astype(jnp.int32), scaled).astype(jnp.int16)


def unpack(coded):
    wide = coded.astype(jnp.int32).astype(jnp.float32)
    return wide * jnp.exp2(wide[BLK + 1 : BLK + 2] - BITS)


def batch_kernel(
    count,
    blocks_in,
    basis_in,
    turned_in,
    core,
    weights,
    density,
    pieces_out,
    blocks,
    basis,
    turned,
    pieces,
    both,
    total,
    scaled,
    arrived,
    left_here,
):
    def chunk(k):
        at = (slice(None), slice(k * CHUNK, (k + 1) * CHUNK))
        return pltpu.make_async_copy(basis_in.at[at], basis.at[at], arrived.at[k])

    chunks = [chunk(k) for k in range(COLS // CHUNK)]
    load_blocks = pltpu.make_async_copy(blocks_in, blocks, arrived.at[len(chunks)])
    load_turned = pltpu.make_async_copy(turned_in, turned, arrived.at[len(chunks) + 1])
    load_blocks.start()
    chunks[0].start()

    rows, cols = row_col((BLK, BLK))

    def message(device):
        return blocks[device].astype(jnp.int32).astype(jnp.float32)

    def place(side, start, right, value):
        top = value.astype(jnp.bfloat16)
        at = pl.ds(start, BLK)
        both[side, at, right * BLK : (right + 1) * BLK] = top
        rest = (value - top.astype(jnp.float32)).astype(jnp.bfloat16)
        both[side, at, PAIR + right * BLK : PAIR + (right + 1) * BLK] = rest

    def place_pair(big, p):
        for di in range(2):
            for dj in range(2):
                device = (2 * p + di) * INNERS + big if di == dj else (2 * big + dj) * INNERS + p
                start = p * PAIR + di * BLK
                place(big % 2, start, dj, message(device)[:BLK])

    def place_diagonal(big):
        first = message(2 * big * INNERS + big)
        second = message((2 * big + 1) * INNERS + big)
        diagonal = jnp.broadcast_to(first[BLK : BLK + 1], (BLK, BLK))
        first, second = first[:BLK], second[:BLK]
        cross = jnp.where(rows > cols, first, jnp.where(rows < cols, second, diagonal))
        side, start = big % 2, big * PAIR
        place(side, start, 0, jnp.where(rows <= cols, first, 0.0))
        place(side, start, 1, cross)
        place(side, start + BLK, 0, jnp.zeros((BLK, BLK), jnp.float32))
        place(side, start + BLK, 1, jnp.where(rows >= cols, second, 0.0))

    load_blocks.wait()
    place_diagonal(0)
    tiles = PTS // TILE
    for big in range(KB // 2):
        depth = (big + 1) * PAIR
        if big * PAIR % CHUNK == 0:
            k = big * PAIR // CHUNK
            chunks[k].wait()
            if k + 1 < len(chunks):
                chunks[k + 1].start()
            else:
                load_turned.start()

        if big + 1 < KB // 2:
            for p in range(big + 1):
                place_pair(big + 1, p)
        for m in range(tiles):
            at = slice(m * TILE, (m + 1) * TILE)
            product = jnp.dot(
                basis[at, :depth], both[big % 2, :depth], preferred_element_type=jnp.float32
            )
            product = product[:, :PAIR] + product[:, PAIR:]
            product *= basis[at, big * PAIR : (big + 1) * PAIR].astype(jnp.float32)
            folded = product[:, :BLK] + product[:, BLK:]
            total[at] = folded if big == 0 else total[at] + folded
        if big + 1 < KB // 2:
            place_diagonal(big + 1)

    summed = jnp.sum(total[...], axis=1, keepdims=True) * (1.0 / STEP)
    found = core[...] + summed
    density[...] = found
    potential = slater_factor * jnp.exp(jnp.log(jnp.maximum(found, density_floor)) * (1.0 / 3.0))
    live = lax.broadcasted_iota(jnp.int32, (PTS, 1), 0) < count[0]
    total[...] = jnp.broadcast_to(jnp.where(live, weights[...] * potential, 0.0), (PTS, BLK))

    tail = jnp.zeros((ROWS - BLK, BLK), jnp.float32)

    def send(device, value, last=tail):
        pieces[device] = pack(jnp.concatenate([value, last], axis=0))
        pltpu.make_async_copy(pieces.at[device], pieces_out.at[device], left_here).start()

    load_turned.wait()
    for big in range(KB // 2):
        half = big % 2
        for k in range(2):
            lanes = slice(big * PAIR + k * BLK, big * PAIR + (k + 1) * BLK)
            part_of = (total[...] * basis[:, lanes].astype(jnp.float32)).astype(jnp.bfloat16)
            scaled[half, :, k * BLK : (k + 1) * BLK] = part_of
        products = jnp.dot(
            turned[: (big + 1) * PAIR], scaled[half], preferred_element_type=jnp.float32
        )
        for part in range(big + 1):
            product = products[part * PAIR : (part + 1) * PAIR]
            i, j = 2 * part, 2 * big
            if part < big:
                for di in range(2):
                    for dj in range(2):
                        send(
                            owner(i + di, j + dj),
                            product[di * BLK : (di + 1) * BLK, dj * BLK : (dj + 1) * BLK],
                        )
            else:
                cross = product[:BLK, BLK:]
                diagonal = jnp.sum(jnp.where(rows == cols, cross, 0.0), axis=0, keepdims=True)
                last = jnp.broadcast_to(diagonal, (ROWS - BLK, BLK))
                send(i * INNERS + big, jnp.where(rows > cols, cross, product[:BLK, :BLK]), last)
                send((i + 1) * INNERS + big, jnp.where(rows < cols, cross, product[BLK:, BLK:]), last)
    pltpu.make_async_copy(pieces, pieces_out, left_here).wait()


def batch(count, blocks, basis, turned, core, weights):
    vmem = pl.BlockSpec(memory_space=pltpu.VMEM)
    anywhere = pl.BlockSpec(memory_space=pl.ANY)
    messages = (DEVICES, ROWS, BLK)
    return pl.pallas_call(
        batch_kernel,
        out_shape=(
            jax.ShapeDtypeStruct((PTS, 1), jnp.float32),
            jax.ShapeDtypeStruct(messages, jnp.int16),
        ),
        in_specs=[pl.BlockSpec(memory_space=pltpu.SMEM)] + [anywhere] * 3 + [vmem] * 2,
        out_specs=(vmem, pl.BlockSpec(memory_space=pltpu.HBM)),
        scratch_shapes=[
            pltpu.VMEM(messages, jnp.int16),
            pltpu.VMEM((PTS, COLS), jnp.bfloat16),
            pltpu.VMEM((COLS, PTS), jnp.bfloat16),
            pltpu.VMEM(messages, jnp.int16),
            pltpu.VMEM((2, COLS, 2 * PAIR), jnp.bfloat16),
            pltpu.VMEM((PTS, BLK), jnp.float32),
            pltpu.VMEM((2, PTS, PAIR), jnp.bfloat16),
            pltpu.SemaphoreType.DMA((COLS // CHUNK + 2,)),
            pltpu.SemaphoreType.DMA,
        ],
        compiler_params=pltpu.CompilerParams(vmem_limit_bytes=VMEM_ALL),
    )(count, blocks, basis, turned, core, weights)


def sum_kernel(index, pieces, total, copy):
    step = pl.program_id(0)
    per_step = pieces.shape[0]

    @pl.when(step == 0)
    def _():
        total[...] = jnp.zeros_like(total)

    def add(k, carry):
        at = index[step * per_step + k]
        total[at] = total[at] + unpack(pieces[k])
        return carry

    lax.fori_loop(0, per_step, add, 0, unroll=4)

    @pl.when(step == pl.num_programs(0) - 1)
    def _():
        for k in range(BUCKETS):
            copy[k] = pack(total[k])


def sum_pieces(index, pieces):
    per_step = 16
    shape = (BUCKETS, ROWS, BLK)
    whole = pl.BlockSpec(shape, lambda s: (0, 0, 0))
    return pl.pallas_call(
        sum_kernel,
        grid=(DEVICES // per_step,),
        out_shape=(jax.ShapeDtypeStruct(shape, jnp.float32), jax.ShapeDtypeStruct(shape, jnp.int16)),
        in_specs=[
            pl.BlockSpec(memory_space=pltpu.SMEM),
            pl.BlockSpec((per_step, ROWS, BLK), lambda s: (s, 0, 0)),
        ],
        out_specs=(whole, whole),
        compiler_params=pltpu.CompilerParams(vmem_limit_bytes=VMEM_SMALL),
    )(index, pieces)


def finish_kernel(flags, total, mirror, out):
    flip = flags[0] == 1
    special = flags[1] == 1
    half = flags[3]
    rows, cols = row_col((BLK, BLK))

    def slot(which, a, b):
        start = pl.multiple_of(which * SLOT + b * BLK, BLK)
        return (slice(a * BLK, (a + 1) * BLK), pl.ds(start, BLK))

    def received(k):
        return unpack(mirror[k])

    @pl.when(jnp.logical_not(special))
    def _():
        for a in range(SPAN):
            for b in range(SPAN):
                k = a * SPAN + b

                @pl.when(flip)
                def _():
                    out[slot(half, b, a)] = total[k, :BLK].T
                    out[slot(1 - half, b, a)] = received(k)[:BLK].T

                @pl.when(jnp.logical_not(flip))
                def _():
                    out[slot(half, a, b)] = total[k, :BLK]
                    out[slot(1 - half, a, b)] = received(k)[:BLK]

    def diagonal_group(lower):
        for a in range(SPAN):
            for b in range(SPAN):
                k = a * SPAN + b
                mine, theirs = total[k], received(k)
                first, second = (mine, theirs) if lower else (theirs, mine)
                middle = jnp.broadcast_to(first[BLK : BLK + 1], (BLK, BLK))
                cross = jnp.where(
                    rows > cols, first[:BLK], jnp.where(rows < cols, second[:BLK], middle)
                )
                if lower:
                    out[slot(half, a, b)] = cross
                else:
                    out[slot(half, b, a)] = cross.T
                if a != b:
                    out[slot(1 - half, a, b)] = jnp.zeros((BLK, BLK), jnp.float32)
        for a in range(SPAN):
            held = jnp.zeros((BLK, BLK), jnp.float32)
            for b in range(SPAN):
                held += total[a * SPAN + b if lower else b * SPAN + a, :BLK]
            keep = rows < cols if lower else rows > cols
            strict = jnp.where(keep, held, 0.0)
            out[slot(1 - half, a, a)] = jnp.where(rows == cols, held, strict + strict.T)

    @pl.when(jnp.logical_and(special, flags[2] == 1))
    def _():
        diagonal_group(True)

    @pl.when(jnp.logical_and(special, flags[2] == 0))
    def _():
        diagonal_group(False)


def finish(flags, total, mirror):
    vmem = pl.BlockSpec(memory_space=pltpu.VMEM)
    return pl.pallas_call(
        finish_kernel,
        out_shape=jax.ShapeDtypeStruct((SLOT, 2 * SLOT), jnp.float32),
        in_specs=[pl.BlockSpec(memory_space=pltpu.SMEM), vmem, vmem],
        out_specs=vmem,
        compiler_params=pltpu.CompilerParams(vmem_limit_bytes=VMEM_SMALL),
    )(flags, total, mirror)


def per_device(density_matrix, basis_values, block_list, point_counts, core_density, grid_weights):
    g = lax.axis_index("group")
    n = lax.axis_index("inner")
    odd = lax.rem(g, 2)
    half = jnp.where(g < 2 * n, odd, 1 - odd)
    flip = (g > 2 * n).astype(jnp.int32)
    special = g // 2 == n
    column_slot = 2 * n + half
    first, second = jnp.minimum(g, column_slot), jnp.maximum(g, column_slot)
    flags = jnp.stack([flip, special.astype(jnp.int32), 1 - odd, half]).astype(jnp.int32)
    pairs = mirror_pairs()

    basis = basis_values[0]
    left, right = density_matrix[:, :SLOT], density_matrix[:, SLOT:]
    sent = jnp.where((half == 0) == special, left, right)
    mirror = lax.ppermute(sent, AXES, pairs)
    lists = lax.all_to_all(
        jnp.broadcast_to(block_list, (DEVICES, KB)), AXES, split_axis=0, concat_axis=0, tiled=True
    )
    slots = jnp.arange(KB, dtype=jnp.int32)
    factor = jnp.where(slots == first, SPAN, 0) + jnp.where(slots == second, 1, 0)
    index = jnp.sum((lists - slots * SPAN) * factor, axis=1).astype(jnp.int32)

    picked = pick(flags, index, density_matrix, mirror)
    blocks = lax.all_to_all(picked, AXES, split_axis=0, concat_axis=0, tiled=True)
    density, pieces = batch(
        point_counts,
        blocks,
        basis,
        basis.T,
        core_density.reshape(PTS, 1),
        grid_weights.reshape(PTS, 1),
    )
    landed = lax.all_to_all(pieces, AXES, split_axis=0, concat_axis=0, tiled=True)
    total, copy = sum_pieces(index, landed)
    returned = lax.ppermute(copy, AXES, [(target, source) for source, target in pairs])
    return density.reshape(1, PTS), finish(flags, total, returned)


def solution(mesh):
    return jax.shard_map(
        per_device,
        mesh=mesh,
        in_specs=(
            P("group", "inner"),
            P(AXES, None, None),
            P(AXES, None),
            P(AXES),
            P(AXES, None),
            P(AXES, None),
        ),
        out_specs=(P(AXES, None), P("group", "inner")),
        check_vma=False,
    )
```

```python
import jax
import jax.numpy as jnp
from jax import lax
from jax.experimental import pallas as pl
from jax.experimental.pallas import tpu as pltpu
from jax.sharding import PartitionSpec as P

BLK = 128
KB = 16
GROUPS = 16
INNERS = 8
DEVICES = GROUPS * INNERS
SPAN = 4
SLOT = SPAN * BLK
BUCKETS = SPAN * SPAN
ROWS = BLK + 8
PTS = 1536
COLS = KB * BLK
PAIR = 2 * BLK
AXES = ("group", "inner")

slater_factor = -((3.0 / 3.141592653589793) ** (1.0 / 3.0))
density_floor = 0.1
STEP = float(2**22)
BITS = 14.0
TINY = 2.0**-100
TILE = 256
CHUNK = 512
VMEM_ALL = 60 * 2**20
VMEM_SMALL = 24 * 2**20


def owner(i, j):
    return i * INNERS + j // 2 if (i + j) % 2 == 0 else j * INNERS + i // 2


def chosen_half(g, n):
    odd = g % 2
    return odd if g < 2 * n else 1 - odd


def mirror_pairs():
    pairs = []
    for g in range(GROUPS):
        for n in range(INNERS):
            half = chosen_half(g, n)
            if g // 2 != n:
                half = 1 - half
            pairs.append((g * INNERS + n, (2 * n + half) * INNERS + g // 2))
    return pairs


def row_col(shape):
    return lax.broadcasted_iota(jnp.int32, shape, 0), lax.broadcasted_iota(jnp.int32, shape, 1)


def encode(value):
    return jnp.floor(value * STEP + 0.5).astype(jnp.int32).astype(jnp.int16)


def pick_kernel(flags, index, matrix, mirror, out, table):
    step = pl.program_id(0)
    per_step = out.shape[0]

    @pl.when(step == 0)
    def _():
        flip = flags[0] == 1
        special = flags[1] == 1
        low = flags[2] == 1
        own_start = flags[3] * SLOT
        other_start = SLOT - own_start

        def put(a, b, first, second):
            rows, cols = row_col((BLK, BLK))
            total = first + second.T
            diagonal = jnp.sum(jnp.where(rows == cols, total, 0.0), axis=0, keepdims=True)
            tail = jnp.broadcast_to(diagonal, (ROWS - BLK, BLK))
            table[a * SPAN + b] = encode(jnp.concatenate([total, tail], axis=0))

            @pl.when(special)
            def _():
                at = jnp.where(low, a, b)
                start = pl.multiple_of(at * BLK, BLK)
                side = pl.multiple_of(other_start + at * BLK, BLK)
                block = matrix[pl.ds(start, BLK), pl.ds(side, BLK)].astype(jnp.float32)
                both = jnp.where(rows == cols, block, block + block.T)
                keep = jnp.where(low, rows - cols, cols - rows) > 0
                packed = jnp.where(keep, total, both)
                table[a * SPAN + b] = encode(jnp.concatenate([packed, tail], axis=0))

        def mirror_block(a, b):
            return mirror[a * BLK : (a + 1) * BLK, b * BLK : (b + 1) * BLK].astype(jnp.float32)

        def own_block(a, b):
            start = pl.multiple_of(own_start + b * BLK, BLK)
            return matrix[a * BLK : (a + 1) * BLK, pl.ds(start, BLK)].astype(jnp.float32)

        for a in range(SPAN):
            for b in range(SPAN):

                @pl.when(flip)
                def _():
                    put(a, b, mirror_block(a, b), own_block(b, a))

                @pl.when(jnp.logical_not(flip))
                def _():
                    put(a, b, own_block(a, b), mirror_block(b, a))

    def copy(k, carry):
        out[k] = table[index[step * per_step + k]]
        return carry

    lax.fori_loop(0, per_step, copy, 0, unroll=4)


def pick(flags, index, matrix, mirror):
    per_step = 16
    return pl.pallas_call(
        pick_kernel,
        grid=(DEVICES // per_step,),
        out_shape=jax.ShapeDtypeStruct((DEVICES, ROWS, BLK), jnp.int16),
        in_specs=[
            pl.BlockSpec(memory_space=pltpu.SMEM),
            pl.BlockSpec(memory_space=pltpu.SMEM),
            pl.BlockSpec((SLOT, 2 * SLOT), lambda s: (0, 0)),
            pl.BlockSpec((SLOT, SLOT), lambda s: (0, 0)),
        ],
        out_specs=pl.BlockSpec((per_step, ROWS, BLK), lambda s: (s, 0, 0)),
        scratch_shapes=[pltpu.VMEM((BUCKETS, ROWS, BLK), jnp.int16)],
        compiler_params=pltpu.CompilerParams(vmem_limit_bytes=VMEM_SMALL),
    )(flags, index, matrix, mirror)


def pack(value):
    most = jnp.max(jnp.abs(value), axis=0, keepdims=True)
    power = jnp.ceil(jnp.log2(jnp.maximum(most, TINY)))
    scaled = jnp.floor(value * jnp.exp2(BITS - power) + 0.5).astype(jnp.int32)
    rows, _ = row_col(value.shape)
    return jnp.where(rows > BLK, power.astype(jnp.int32), scaled).astype(jnp.int16)


def unpack(coded):
    wide = coded.astype(jnp.int32).astype(jnp.float32)
    return wide * jnp.exp2(wide[BLK + 1 : BLK + 2] - BITS)


def batch_kernel(
    count,
    blocks_in,
    basis_in,
    coarse_in,
    turned_in,
    core,
    weights,
    density,
    pieces_out,
    blocks,
    basis,
    coarse,
    turned,
    pieces,
    high,
    fine,
    total,
    scaled,
    arrived,
    left_here,
):
    def chunk(k, source, target, at):
        lanes = (slice(None), slice(k * CHUNK, (k + 1) * CHUNK))
        return pltpu.make_async_copy(source.at[lanes], target.at[lanes], arrived.at[at])

    chunks = []
    for k in range(COLS // CHUNK):
        chunks.append(chunk(k, basis_in, basis, 2 * k))
        chunks.append(chunk(k, coarse_in, coarse, 2 * k + 1))
    load_blocks = pltpu.make_async_copy(blocks_in, blocks, arrived.at[len(chunks)])
    load_turned = pltpu.make_async_copy(turned_in, turned, arrived.at[len(chunks) + 1])
    load_blocks.start()
    chunks[0].start()
    chunks[1].start()

    rows, cols = row_col((BLK, BLK))

    def message(device):
        return blocks[device].astype(jnp.int32).astype(jnp.float32)

    def place(side, start, right, value):
        top = value.astype(jnp.bfloat16)
        at = pl.ds(start, BLK)
        high[side, at, right * BLK : (right + 1) * BLK] = top
        rest = (value - top.astype(jnp.float32)).astype(jnp.float8_e4m3fn)
        fine[side, at, right * BLK : (right + 1) * BLK] = rest

    def place_pair(big, p):
        for di in range(2):
            for dj in range(2):
                device = (2 * p + di) * INNERS + big if di == dj else (2 * big + dj) * INNERS + p
                start = p * PAIR + di * BLK
                place(big % 2, start, dj, message(device)[:BLK])

    def place_diagonal(big):
        first = message(2 * big * INNERS + big)
        second = message((2 * big + 1) * INNERS + big)
        diagonal = jnp.broadcast_to(first[BLK : BLK + 1], (BLK, BLK))
        first, second = first[:BLK], second[:BLK]
        cross = jnp.where(rows > cols, first, jnp.where(rows < cols, second, diagonal))
        side, start = big % 2, big * PAIR
        place(side, start, 0, jnp.where(rows <= cols, first, 0.0))
        place(side, start, 1, cross)
        place(side, start + BLK, 0, jnp.zeros((BLK, BLK), jnp.float32))
        place(side, start + BLK, 1, jnp.where(rows >= cols, second, 0.0))

    load_blocks.wait()
    place_diagonal(0)
    tiles = PTS // TILE
    for big in range(KB // 2):
        depth = (big + 1) * PAIR
        if big * PAIR % CHUNK == 0:
            k = 2 * (big * PAIR // CHUNK)
            chunks[k].wait()
            chunks[k + 1].wait()
            if k + 2 < len(chunks):
                chunks[k + 2].start()
                chunks[k + 3].start()
            else:
                load_turned.start()

        for m in range(tiles):
            if big + 1 < KB // 2:
                for p in range(m, big + 1, tiles):
                    place_pair(big + 1, p)
            at = slice(m * TILE, (m + 1) * TILE)
            side = big % 2
            product = jnp.dot(basis[at, :depth], high[side, :depth], preferred_element_type=jnp.float32)
            product += jnp.dot(coarse[at, :depth], fine[side, :depth], preferred_element_type=jnp.float32)
            product *= basis[at, big * PAIR : (big + 1) * PAIR].astype(jnp.float32)
            folded = product[:, :BLK] + product[:, BLK:]
            total[at] = folded if big == 0 else total[at] + folded
        if big + 1 < KB // 2:
            place_diagonal(big + 1)

    summed = jnp.sum(total[...], axis=1, keepdims=True) * (1.0 / STEP)
    found = core[...] + summed
    density[...] = found
    potential = slater_factor * jnp.exp(jnp.log(jnp.maximum(found, density_floor)) * (1.0 / 3.0))
    live = lax.broadcasted_iota(jnp.int32, (PTS, 1), 0) < count[0]
    total[...] = jnp.broadcast_to(jnp.where(live, weights[...] * potential, 0.0), (PTS, BLK))

    tail = jnp.zeros((ROWS - BLK, BLK), jnp.float32)

    def send(device, value, last=tail):
        pieces[device] = pack(jnp.concatenate([value, last], axis=0))
        pltpu.make_async_copy(pieces.at[device], pieces_out.at[device], left_here).start()

    def weigh(big, low, high_end):
        for k in range(2):
            lanes = slice(big * PAIR + k * BLK, big * PAIR + (k + 1) * BLK)
            at = slice(low, high_end)
            part_of = (total[at] * basis[at, lanes].astype(jnp.float32)).astype(jnp.bfloat16)
            scaled[big % 2, at, k * BLK : (k + 1) * BLK] = part_of

    weigh(0, 0, PTS)
    load_turned.wait()
    for big in range(KB // 2):
        cuts = [PTS // 16 * k // (big + 1) * 16 for k in range(big + 2)]
        for part in range(big + 1):
            product = jnp.dot(
                turned[part * PAIR : (part + 1) * PAIR], scaled[big % 2], preferred_element_type=jnp.float32
            )
            if big + 1 < KB // 2:
                weigh(big + 1, cuts[part], cuts[part + 1])
            i, j = 2 * part, 2 * big
            if part < big:
                for di in range(2):
                    for dj in range(2):
                        send(
                            owner(i + di, j + dj),
                            product[di * BLK : (di + 1) * BLK, dj * BLK : (dj + 1) * BLK],
                        )
            else:
                cross = product[:BLK, BLK:]
                diagonal = jnp.sum(jnp.where(rows == cols, cross, 0.0), axis=0, keepdims=True)
                last = jnp.broadcast_to(diagonal, (ROWS - BLK, BLK))
                send(i * INNERS + big, jnp.where(rows > cols, cross, product[:BLK, :BLK]), last)
                send((i + 1) * INNERS + big, jnp.where(rows < cols, cross, product[BLK:, BLK:]), last)
    pltpu.make_async_copy(pieces, pieces_out, left_here).wait()


def batch(count, blocks, basis, coarse, turned, core, weights):
    vmem = pl.BlockSpec(memory_space=pltpu.VMEM)
    anywhere = pl.BlockSpec(memory_space=pl.ANY)
    messages = (DEVICES, ROWS, BLK)
    return pl.pallas_call(
        batch_kernel,
        out_shape=(
            jax.ShapeDtypeStruct((PTS, 1), jnp.float32),
            jax.ShapeDtypeStruct(messages, jnp.int16),
        ),
        in_specs=[pl.BlockSpec(memory_space=pltpu.SMEM)] + [anywhere] * 4 + [vmem] * 2,
        out_specs=(vmem, pl.BlockSpec(memory_space=pltpu.HBM)),
        scratch_shapes=[
            pltpu.VMEM(messages, jnp.int16),
            pltpu.VMEM((PTS, COLS), jnp.bfloat16),
            pltpu.VMEM((PTS, COLS), jnp.float8_e4m3fn),
            pltpu.VMEM((COLS, PTS), jnp.bfloat16),
            pltpu.VMEM(messages, jnp.int16),
            pltpu.VMEM((2, COLS, PAIR), jnp.bfloat16),
            pltpu.VMEM((2, COLS, PAIR), jnp.float8_e4m3fn),
            pltpu.VMEM((PTS, BLK), jnp.float32),
            pltpu.VMEM((2, PTS, PAIR), jnp.bfloat16),
            pltpu.SemaphoreType.DMA((2 * (COLS // CHUNK) + 2,)),
            pltpu.SemaphoreType.DMA,
        ],
        compiler_params=pltpu.CompilerParams(vmem_limit_bytes=VMEM_ALL),
    )(count, blocks, basis, coarse, turned, core, weights)


def sum_kernel(index, pieces, total, copy):
    step = pl.program_id(0)
    per_step = pieces.shape[0]

    @pl.when(step == 0)
    def _():
        total[...] = jnp.zeros_like(total)

    def add(k, carry):
        at = index[step * per_step + k]
        total[at] = total[at] + unpack(pieces[k])
        return carry

    lax.fori_loop(0, per_step, add, 0, unroll=4)

    @pl.when(step == pl.num_programs(0) - 1)
    def _():
        for k in range(BUCKETS):
            copy[k] = pack(total[k])


def sum_pieces(index, pieces):
    per_step = 16
    shape = (BUCKETS, ROWS, BLK)
    whole = pl.BlockSpec(shape, lambda s: (0, 0, 0))
    return pl.pallas_call(
        sum_kernel,
        grid=(DEVICES // per_step,),
        out_shape=(jax.ShapeDtypeStruct(shape, jnp.float32), jax.ShapeDtypeStruct(shape, jnp.int16)),
        in_specs=[
            pl.BlockSpec(memory_space=pltpu.SMEM),
            pl.BlockSpec((per_step, ROWS, BLK), lambda s: (s, 0, 0)),
        ],
        out_specs=(whole, whole),
        compiler_params=pltpu.CompilerParams(vmem_limit_bytes=VMEM_SMALL),
    )(index, pieces)


def finish_kernel(flags, total, mirror, out):
    flip = flags[0] == 1
    special = flags[1] == 1
    half = flags[3]
    rows, cols = row_col((BLK, BLK))

    def slot(which, a, b):
        start = pl.multiple_of(which * SLOT + b * BLK, BLK)
        return (slice(a * BLK, (a + 1) * BLK), pl.ds(start, BLK))

    def received(k):
        return unpack(mirror[k])

    @pl.when(jnp.logical_not(special))
    def _():
        for a in range(SPAN):
            for b in range(SPAN):
                k = a * SPAN + b

                @pl.when(flip)
                def _():
                    out[slot(half, b, a)] = total[k, :BLK].T
                    out[slot(1 - half, b, a)] = received(k)[:BLK].T

                @pl.when(jnp.logical_not(flip))
                def _():
                    out[slot(half, a, b)] = total[k, :BLK]
                    out[slot(1 - half, a, b)] = received(k)[:BLK]

    def diagonal_group(lower):
        for a in range(SPAN):
            for b in range(SPAN):
                k = a * SPAN + b
                mine, theirs = total[k], received(k)
                first, second = (mine, theirs) if lower else (theirs, mine)
                middle = jnp.broadcast_to(first[BLK : BLK + 1], (BLK, BLK))
                cross = jnp.where(
                    rows > cols, first[:BLK], jnp.where(rows < cols, second[:BLK], middle)
                )
                if lower:
                    out[slot(half, a, b)] = cross
                else:
                    out[slot(half, b, a)] = cross.T
                if a != b:
                    out[slot(1 - half, a, b)] = jnp.zeros((BLK, BLK), jnp.float32)
        for a in range(SPAN):
            held = jnp.zeros((BLK, BLK), jnp.float32)
            for b in range(SPAN):
                held += total[a * SPAN + b if lower else b * SPAN + a, :BLK]
            keep = rows < cols if lower else rows > cols
            strict = jnp.where(keep, held, 0.0)
            out[slot(1 - half, a, a)] = jnp.where(rows == cols, held, strict + strict.T)

    @pl.when(jnp.logical_and(special, flags[2] == 1))
    def _():
        diagonal_group(True)

    @pl.when(jnp.logical_and(special, flags[2] == 0))
    def _():
        diagonal_group(False)


def finish(flags, total, mirror):
    vmem = pl.BlockSpec(memory_space=pltpu.VMEM)
    return pl.pallas_call(
        finish_kernel,
        out_shape=jax.ShapeDtypeStruct((SLOT, 2 * SLOT), jnp.float32),
        in_specs=[pl.BlockSpec(memory_space=pltpu.SMEM), vmem, vmem],
        out_specs=vmem,
        compiler_params=pltpu.CompilerParams(vmem_limit_bytes=VMEM_SMALL),
    )(flags, total, mirror)


def per_device(density_matrix, basis_values, block_list, point_counts, core_density, grid_weights):
    g = lax.axis_index("group")
    n = lax.axis_index("inner")
    odd = lax.rem(g, 2)
    half = jnp.where(g < 2 * n, odd, 1 - odd)
    flip = (g > 2 * n).astype(jnp.int32)
    special = g // 2 == n
    column_slot = 2 * n + half
    first, second = jnp.minimum(g, column_slot), jnp.maximum(g, column_slot)
    flags = jnp.stack([flip, special.astype(jnp.int32), 1 - odd, half]).astype(jnp.int32)
    pairs = mirror_pairs()

    basis = basis_values[0]
    left, right = density_matrix[:, :SLOT], density_matrix[:, SLOT:]
    sent = jnp.where((half == 0) == special, left, right)
    mirror = lax.ppermute(sent, AXES, pairs)
    lists = lax.all_to_all(
        jnp.broadcast_to(block_list, (DEVICES, KB)), AXES, split_axis=0, concat_axis=0, tiled=True
    )
    slots = jnp.arange(KB, dtype=jnp.int32)
    factor = jnp.where(slots == first, SPAN, 0) + jnp.where(slots == second, 1, 0)
    index = jnp.sum((lists - slots * SPAN) * factor, axis=1).astype(jnp.int32)

    picked = pick(flags, index, density_matrix, mirror)
    blocks = lax.all_to_all(picked, AXES, split_axis=0, concat_axis=0, tiled=True)
    density, pieces = batch(
        point_counts,
        blocks,
        basis,
        basis.astype(jnp.float8_e4m3fn),
        basis.T,
        core_density.reshape(PTS, 1),
        grid_weights.reshape(PTS, 1),
    )
    landed = lax.all_to_all(pieces, AXES, split_axis=0, concat_axis=0, tiled=True)
    total, copy = sum_pieces(index, landed)
    returned = lax.ppermute(copy, AXES, [(target, source) for source, target in pairs])
    return density.reshape(1, PTS), finish(flags, total, returned)


def solution(mesh):
    return jax.shard_map(
        per_device,
        mesh=mesh,
        in_specs=(
            P("group", "inner"),
            P(AXES, None, None),
            P(AXES, None),
            P(AXES),
            P(AXES, None),
            P(AXES, None),
        ),
        out_specs=(P(AXES, None), P("group", "inner")),
        check_vma=False,
    )
```

```python
import jax
import jax.numpy as jnp
from jax import lax
from jax.experimental import pallas as pl
from jax.experimental.pallas import tpu as pltpu
from jax.sharding import PartitionSpec as P

BLK = 128
KB = 16
GROUPS = 16
INNERS = 8
DEVICES = GROUPS * INNERS
SPAN = 4
SLOT = SPAN * BLK
BUCKETS = SPAN * SPAN
ROWS = BLK + 8
PTS = 1536
COLS = KB * BLK
PAIR = 2 * BLK
AXES = ("group", "inner")

slater_factor = -((3.0 / 3.141592653589793) ** (1.0 / 3.0))
density_floor = 0.1
STEP = float(2**22)
BITS = 14.0
TINY = 2.0**-100
TILE = 256
CHUNK = 512
VMEM_BATCH = 38 * 2**20
VMEM_SMALL = 24 * 2**20


def owner(i, j):
    return i * INNERS + j // 2 if (i + j) % 2 == 0 else j * INNERS + i // 2


def chosen_half(g, n):
    odd = g % 2
    return odd if g < 2 * n else 1 - odd


def mirror_pairs():
    pairs = []
    for g in range(GROUPS):
        for n in range(INNERS):
            half = chosen_half(g, n)
            if g // 2 != n:
                half = 1 - half
            pairs.append((g * INNERS + n, (2 * n + half) * INNERS + g // 2))
    return pairs


def row_col(shape):
    return lax.broadcasted_iota(jnp.int32, shape, 0), lax.broadcasted_iota(jnp.int32, shape, 1)


def encode(value):
    return jnp.floor(value * STEP + 0.5).astype(jnp.int32).astype(jnp.int16)


def pick_kernel(flags, index, own, other, mirror, out, table):
    step = pl.program_id(0)
    per_step = out.shape[0]

    @pl.when(step == 0)
    def _():
        flip = flags[0] == 1
        special = flags[1] == 1
        low = flags[2] == 1

        def put(a, b, first, second):
            rows, cols = row_col((BLK, BLK))
            total = first + second.T
            diagonal = jnp.sum(jnp.where(rows == cols, total, 0.0), axis=0, keepdims=True)
            tail = jnp.broadcast_to(diagonal, (ROWS - BLK, BLK))
            table[a * SPAN + b] = encode(jnp.concatenate([total, tail], axis=0))

            @pl.when(special)
            def _():
                at = jnp.where(low, a, b)
                start = pl.multiple_of(at * BLK, BLK)
                block = other[pl.ds(start, BLK), pl.ds(start, BLK)].astype(jnp.float32)
                both = jnp.where(rows == cols, block, block + block.T)
                keep = jnp.where(low, rows - cols, cols - rows) > 0
                packed = jnp.where(keep, total, both)
                table[a * SPAN + b] = encode(jnp.concatenate([packed, tail], axis=0))

        def block_of(ref, a, b):
            return ref[a * BLK : (a + 1) * BLK, b * BLK : (b + 1) * BLK].astype(jnp.float32)

        for a in range(SPAN):
            for b in range(SPAN):

                @pl.when(flip)
                def _():
                    put(a, b, block_of(mirror, a, b), block_of(own, b, a))

                @pl.when(jnp.logical_not(flip))
                def _():
                    put(a, b, block_of(own, a, b), block_of(mirror, b, a))

    def copy(k, carry):
        out[k] = table[index[step * per_step + k]]
        return carry

    lax.fori_loop(0, per_step, copy, 0, unroll=4)


def pick(flags, index, own, other, mirror):
    per_step = 16
    whole = pl.BlockSpec((SLOT, SLOT), lambda s: (0, 0))
    return pl.pallas_call(
        pick_kernel,
        grid=(DEVICES // per_step,),
        out_shape=jax.ShapeDtypeStruct((DEVICES, ROWS, BLK), jnp.int16),
        in_specs=[
            pl.BlockSpec(memory_space=pltpu.SMEM),
            pl.BlockSpec(memory_space=pltpu.SMEM),
            whole,
            whole,
            whole,
        ],
        out_specs=pl.BlockSpec((per_step, ROWS, BLK), lambda s: (s, 0, 0)),
        scratch_shapes=[pltpu.VMEM((BUCKETS, ROWS, BLK), jnp.int16)],
        compiler_params=pltpu.CompilerParams(vmem_limit_bytes=VMEM_SMALL),
    )(flags, index, own, other, mirror)


def pack(value):
    most = jnp.max(jnp.abs(value), axis=0, keepdims=True)
    power = jnp.ceil(jnp.log2(jnp.maximum(most, TINY)))
    scaled = jnp.floor(value * jnp.exp2(BITS - power) + 0.5).astype(jnp.int32)
    rows, _ = row_col(value.shape)
    return jnp.where(rows > BLK, power.astype(jnp.int32), scaled).astype(jnp.int16)


def unpack(coded):
    wide = coded.astype(jnp.int32).astype(jnp.float32)
    return wide * jnp.exp2(wide[BLK + 1 : BLK + 2] - BITS)


def batch_kernel(
    count,
    blocks_in,
    basis_in,
    coarse,
    turned_in,
    core_in,
    weights_in,
    density,
    pieces,
    blocks,
    basis,
    turned,
    core,
    weights,
    high,
    fine,
    total,
    scaled,
    arrived,
):
    def chunk(k, source, target, at):
        lanes = (slice(None), slice(k * CHUNK, (k + 1) * CHUNK))
        return pltpu.make_async_copy(source.at[lanes], target.at[lanes], arrived.at[at])

    chunks = [chunk(k, basis_in, basis, k) for k in range(COLS // CHUNK)]
    load_blocks = pltpu.make_async_copy(blocks_in, blocks, arrived.at[len(chunks)])
    load_turned = pltpu.make_async_copy(turned_in, turned, arrived.at[len(chunks) + 1])
    load_core = pltpu.make_async_copy(core_in, core, arrived.at[len(chunks) + 2])
    load_weights = pltpu.make_async_copy(weights_in, weights, arrived.at[len(chunks) + 3])
    load_blocks.start()
    chunks[0].start()

    rows, cols = row_col((BLK, BLK))

    def message(device):
        return blocks[device].astype(jnp.int32).astype(jnp.float32)

    def place(side, start, right, value):
        top = value.astype(jnp.bfloat16)
        at = pl.ds(start, BLK)
        high[side, at, right * BLK : (right + 1) * BLK] = top
        rest = (value - top.astype(jnp.float32)).astype(jnp.float8_e4m3fn)
        fine[side, at, right * BLK : (right + 1) * BLK] = rest

    def place_pair(big, p):
        for di in range(2):
            for dj in range(2):
                device = (2 * p + di) * INNERS + big if di == dj else (2 * big + dj) * INNERS + p
                start = p * PAIR + di * BLK
                place(big % 2, start, dj, message(device)[:BLK])

    def place_diagonal(big):
        first = message(2 * big * INNERS + big)
        second = message((2 * big + 1) * INNERS + big)
        diagonal = jnp.broadcast_to(first[BLK : BLK + 1], (BLK, BLK))
        first, second = first[:BLK], second[:BLK]
        cross = jnp.where(rows > cols, first, jnp.where(rows < cols, second, diagonal))
        side, start = big % 2, big * PAIR
        place(side, start, 0, jnp.where(rows <= cols, first, 0.0))
        place(side, start, 1, cross)
        place(side, start + BLK, 0, jnp.zeros((BLK, BLK), jnp.float32))
        place(side, start + BLK, 1, jnp.where(rows >= cols, second, 0.0))

    load_blocks.wait()
    place_diagonal(0)
    tiles = PTS // TILE
    for big in range(KB // 2):
        depth = (big + 1) * PAIR
        if big * PAIR % CHUNK == 0:
            k = big * PAIR // CHUNK
            chunks[k].wait()
            if k + 1 < len(chunks):
                chunks[k + 1].start()
            else:
                load_core.start()
                load_weights.start()
                load_turned.start()

        for m in range(tiles):
            if big + 1 < KB // 2:
                for p in range(m, big + 1, tiles):
                    place_pair(big + 1, p)
            at = slice(m * TILE, (m + 1) * TILE)
            side = big % 2
            product = jnp.dot(basis[at, :depth], high[side, :depth], preferred_element_type=jnp.float32)
            product += jnp.dot(coarse[at, :depth], fine[side, :depth], preferred_element_type=jnp.float32)
            product *= basis[at, big * PAIR : (big + 1) * PAIR].astype(jnp.float32)
            folded = product[:, :BLK] + product[:, BLK:]
            total[at] = folded if big == 0 else total[at] + folded
        if big + 1 < KB // 2:
            place_diagonal(big + 1)

    summed = jnp.sum(total[...], axis=1, keepdims=True) * (1.0 / STEP)
    load_core.wait()
    load_weights.wait()
    found = core[...] + summed
    density[...] = found
    potential = slater_factor * jnp.exp(jnp.log(jnp.maximum(found, density_floor)) * (1.0 / 3.0))
    live = lax.broadcasted_iota(jnp.int32, (PTS, 1), 0) < count[0]
    total[...] = jnp.broadcast_to(jnp.where(live, weights[...] * potential, 0.0), (PTS, BLK))

    tail = jnp.zeros((ROWS - BLK, BLK), jnp.float32)

    def send(device, value, last=tail):
        pieces[device] = pack(jnp.concatenate([value, last], axis=0))

    def weigh(big, low, high_end):
        for k in range(2):
            lanes = slice(big * PAIR + k * BLK, big * PAIR + (k + 1) * BLK)
            at = slice(low, high_end)
            part_of = (total[at] * basis[at, lanes].astype(jnp.float32)).astype(jnp.bfloat16)
            scaled[big % 2, at, k * BLK : (k + 1) * BLK] = part_of

    weigh(0, 0, PTS)
    load_turned.wait()
    for big in range(KB // 2):
        cuts = [PTS // 16 * k // (big + 1) * 16 for k in range(big + 2)]
        for part in range(big + 1):
            product = jnp.dot(
                turned[part * PAIR : (part + 1) * PAIR], scaled[big % 2], preferred_element_type=jnp.float32
            )
            if big + 1 < KB // 2:
                weigh(big + 1, cuts[part], cuts[part + 1])
            i, j = 2 * part, 2 * big
            if part < big:
                for di in range(2):
                    for dj in range(2):
                        send(
                            owner(i + di, j + dj),
                            product[di * BLK : (di + 1) * BLK, dj * BLK : (dj + 1) * BLK],
                        )
            else:
                cross = product[:BLK, BLK:]
                diagonal = jnp.sum(jnp.where(rows == cols, cross, 0.0), axis=0, keepdims=True)
                last = jnp.broadcast_to(diagonal, (ROWS - BLK, BLK))
                send(i * INNERS + big, jnp.where(rows > cols, cross, product[:BLK, :BLK]), last)
                send((i + 1) * INNERS + big, jnp.where(rows < cols, cross, product[BLK:, BLK:]), last)


def batch(count, blocks, basis, coarse, turned, core, weights):
    vmem = pl.BlockSpec(memory_space=pltpu.VMEM)
    anywhere = pl.BlockSpec(memory_space=pl.ANY)
    messages = (DEVICES, ROWS, BLK)
    return pl.pallas_call(
        batch_kernel,
        out_shape=(
            jax.ShapeDtypeStruct((PTS, 1), jnp.float32),
            jax.ShapeDtypeStruct(messages, jnp.int16),
        ),
        in_specs=[pl.BlockSpec(memory_space=pltpu.SMEM)] + [anywhere, anywhere, vmem, anywhere, anywhere, anywhere],
        out_specs=(vmem, vmem),
        scratch_shapes=[
            pltpu.VMEM(messages, jnp.int16),
            pltpu.VMEM((PTS, COLS), jnp.bfloat16),
            pltpu.VMEM((COLS, PTS), jnp.bfloat16),
            pltpu.VMEM((PTS, 1), jnp.float32),
            pltpu.VMEM((PTS, 1), jnp.float32),
            pltpu.VMEM((2, COLS, PAIR), jnp.bfloat16),
            pltpu.VMEM((2, COLS, PAIR), jnp.float8_e4m3fn),
            pltpu.VMEM((PTS, BLK), jnp.float32),
            pltpu.VMEM((2, PTS, PAIR), jnp.bfloat16),
            pltpu.SemaphoreType.DMA((COLS // CHUNK + 4,)),
        ],
        compiler_params=pltpu.CompilerParams(vmem_limit_bytes=VMEM_BATCH),
    )(count, blocks, basis, coarse, turned, core, weights)


def sum_kernel(index, pieces, total, copy):
    step = pl.program_id(0)
    per_step = pieces.shape[0]

    @pl.when(step == 0)
    def _():
        total[...] = jnp.zeros_like(total)

    def add(k, carry):
        at = index[step * per_step + k]
        total[at] = total[at] + unpack(pieces[k])
        return carry

    lax.fori_loop(0, per_step, add, 0, unroll=4)

    @pl.when(step == pl.num_programs(0) - 1)
    def _():
        for k in range(BUCKETS):
            copy[k] = pack(total[k])


def sum_pieces(index, pieces):
    per_step = 16
    shape = (BUCKETS, ROWS, BLK)
    whole = pl.BlockSpec(shape, lambda s: (0, 0, 0))
    return pl.pallas_call(
        sum_kernel,
        grid=(DEVICES // per_step,),
        out_shape=(jax.ShapeDtypeStruct(shape, jnp.float32), jax.ShapeDtypeStruct(shape, jnp.int16)),
        in_specs=[
            pl.BlockSpec(memory_space=pltpu.SMEM),
            pl.BlockSpec((per_step, ROWS, BLK), lambda s: (s, 0, 0)),
        ],
        out_specs=(whole, whole),
        compiler_params=pltpu.CompilerParams(vmem_limit_bytes=VMEM_SMALL),
    )(index, pieces)


def finish_kernel(flags, total, mirror, out):
    flip = flags[0] == 1
    special = flags[1] == 1
    half = flags[3]
    rows, cols = row_col((BLK, BLK))

    def slot(which, a, b):
        start = pl.multiple_of(which * SLOT + b * BLK, BLK)
        return (slice(a * BLK, (a + 1) * BLK), pl.ds(start, BLK))

    def received(k):
        return unpack(mirror[k])

    @pl.when(jnp.logical_not(special))
    def _():
        for a in range(SPAN):
            for b in range(SPAN):
                k = a * SPAN + b

                @pl.when(flip)
                def _():
                    out[slot(half, b, a)] = total[k, :BLK].T
                    out[slot(1 - half, b, a)] = received(k)[:BLK].T

                @pl.when(jnp.logical_not(flip))
                def _():
                    out[slot(half, a, b)] = total[k, :BLK]
                    out[slot(1 - half, a, b)] = received(k)[:BLK]

    def diagonal_group(lower):
        for a in range(SPAN):
            for b in range(SPAN):
                k = a * SPAN + b
                mine, theirs = total[k], received(k)
                first, second = (mine, theirs) if lower else (theirs, mine)
                middle = jnp.broadcast_to(first[BLK : BLK + 1], (BLK, BLK))
                cross = jnp.where(
                    rows > cols, first[:BLK], jnp.where(rows < cols, second[:BLK], middle)
                )
                if lower:
                    out[slot(half, a, b)] = cross
                else:
                    out[slot(half, b, a)] = cross.T
                if a != b:
                    out[slot(1 - half, a, b)] = jnp.zeros((BLK, BLK), jnp.float32)
        for a in range(SPAN):
            held = jnp.zeros((BLK, BLK), jnp.float32)
            for b in range(SPAN):
                held += total[a * SPAN + b if lower else b * SPAN + a, :BLK]
            keep = rows < cols if lower else rows > cols
            strict = jnp.where(keep, held, 0.0)
            out[slot(1 - half, a, a)] = jnp.where(rows == cols, held, strict + strict.T)

    @pl.when(jnp.logical_and(special, flags[2] == 1))
    def _():
        diagonal_group(True)

    @pl.when(jnp.logical_and(special, flags[2] == 0))
    def _():
        diagonal_group(False)


def finish(flags, total, mirror):
    vmem = pl.BlockSpec(memory_space=pltpu.VMEM)
    return pl.pallas_call(
        finish_kernel,
        out_shape=jax.ShapeDtypeStruct((SLOT, 2 * SLOT), jnp.float32),
        in_specs=[pl.BlockSpec(memory_space=pltpu.SMEM), vmem, vmem],
        out_specs=vmem,
        compiler_params=pltpu.CompilerParams(vmem_limit_bytes=VMEM_SMALL),
    )(flags, total, mirror)


def per_device(density_matrix, basis_values, block_list, point_counts, core_density, grid_weights):
    g = lax.axis_index("group")
    n = lax.axis_index("inner")
    odd = lax.rem(g, 2)
    half = jnp.where(g < 2 * n, odd, 1 - odd)
    flip = (g > 2 * n).astype(jnp.int32)
    special = g // 2 == n
    column_slot = 2 * n + half
    first, second = jnp.minimum(g, column_slot), jnp.maximum(g, column_slot)
    flags = jnp.stack([flip, special.astype(jnp.int32), 1 - odd, half]).astype(jnp.int32)
    pairs = mirror_pairs()

    basis = basis_values[0]
    left, right = density_matrix[:, :SLOT], density_matrix[:, SLOT:]
    own = jnp.where(half == 0, left, right)
    other = jnp.where(half == 0, right, left)
    sent = jnp.where(special, own, other)
    mirror = lax.ppermute(sent, AXES, pairs)
    lists = lax.all_to_all(
        jnp.broadcast_to(block_list, (DEVICES, KB)), AXES, split_axis=0, concat_axis=0, tiled=True
    )
    slots = jnp.arange(KB, dtype=jnp.int32)
    factor = jnp.where(slots == first, SPAN, 0) + jnp.where(slots == second, 1, 0)
    index = jnp.sum((lists - slots * SPAN) * factor, axis=1).astype(jnp.int32)

    picked = pick(flags, index, own, other, mirror)
    blocks = lax.all_to_all(picked, AXES, split_axis=0, concat_axis=0, tiled=True)
    density, pieces = batch(
        point_counts,
        blocks,
        basis,
        basis.astype(jnp.float8_e4m3fn),
        basis.T,
        core_density.reshape(PTS, 1),
        grid_weights.reshape(PTS, 1),
    )
    landed = lax.all_to_all(pieces, AXES, split_axis=0, concat_axis=0, tiled=True)
    total, copy = sum_pieces(index, landed)
    returned = lax.ppermute(copy, AXES, [(target, source) for source, target in pairs])
    return density.reshape(1, PTS), finish(flags, total, returned)


def solution(mesh):
    return jax.shard_map(
        per_device,
        mesh=mesh,
        in_specs=(
            P("group", "inner"),
            P(AXES, None, None),
            P(AXES, None),
            P(AXES),
            P(AXES, None),
            P(AXES, None),
        ),
        out_specs=(P(AXES, None), P("group", "inner")),
        check_vma=False,
    )
```

```python
import jax
import jax.numpy as jnp
from jax import lax
from jax.experimental import pallas as pl
from jax.experimental.pallas import tpu as pltpu
from jax.sharding import PartitionSpec as P

BLK = 128
KB = 16
GROUPS = 16
INNERS = 8
DEVICES = GROUPS * INNERS
SPAN = 4
SLOT = SPAN * BLK
BUCKETS = SPAN * SPAN
ROWS = BLK + 8
PTS = 1536
LINES = PTS // BLK
COLS = KB * BLK
PAIR = 2 * BLK
AXES = ("group", "inner")

slater_factor = -((3.0 / 3.141592653589793) ** (1.0 / 3.0))
density_floor = 0.1
STEP = float(2**22)
BITS = 14.0
TINY = 2.0**-100
TILE = 256
CHUNK = 512
VMEM_BATCH = 38 * 2**20
VMEM_SMALL = 24 * 2**20


def owner(i, j):
    return i * INNERS + j // 2 if (i + j) % 2 == 0 else j * INNERS + i // 2


def chosen_half(g, n):
    odd = g % 2
    return odd if g < 2 * n else 1 - odd


def mirror_pairs():
    pairs = []
    for g in range(GROUPS):
        for n in range(INNERS):
            half = chosen_half(g, n)
            if g // 2 != n:
                half = 1 - half
            pairs.append((g * INNERS + n, (2 * n + half) * INNERS + g // 2))
    return pairs


def row_col(shape):
    return lax.broadcasted_iota(jnp.int32, shape, 0), lax.broadcasted_iota(jnp.int32, shape, 1)


def encode(value):
    return jnp.floor(value * STEP + 0.5).astype(jnp.int32).astype(jnp.int16)


def pick_kernel(flags, index, own, other, mirror, out, table):
    flip = flags[0] == 1
    special = flags[1] == 1
    low = flags[2] == 1

    def put(a, b, first, second):
        rows, cols = row_col((BLK, BLK))
        total = first + second.T
        diagonal = jnp.sum(jnp.where(rows == cols, total, 0.0), axis=0, keepdims=True)
        tail = jnp.broadcast_to(diagonal, (ROWS - BLK, BLK))
        table[a * SPAN + b] = encode(jnp.concatenate([total, tail], axis=0))

        @pl.when(special)
        def _():
            at = jnp.where(low, a, b)
            start = pl.multiple_of(at * BLK, BLK)
            block = other[pl.ds(start, BLK), pl.ds(start, BLK)].astype(jnp.float32)
            both = jnp.where(rows == cols, block, block + block.T)
            keep = jnp.where(low, rows - cols, cols - rows) > 0
            packed = jnp.where(keep, total, both)
            table[a * SPAN + b] = encode(jnp.concatenate([packed, tail], axis=0))

    def block_of(ref, a, b):
        return ref[a * BLK : (a + 1) * BLK, b * BLK : (b + 1) * BLK].astype(jnp.float32)

    for a in range(SPAN):
        for b in range(SPAN):

            @pl.when(flip)
            def _():
                put(a, b, block_of(mirror, a, b), block_of(own, b, a))

            @pl.when(jnp.logical_not(flip))
            def _():
                put(a, b, block_of(own, a, b), block_of(mirror, b, a))

    def copy(k, carry):
        out[k] = table[index[k]]
        return carry

    lax.fori_loop(0, DEVICES, copy, 0, unroll=4)


def pick(flags, index, own, other, mirror):
    vmem = pl.BlockSpec(memory_space=pltpu.VMEM)
    smem = pl.BlockSpec(memory_space=pltpu.SMEM)
    return pl.pallas_call(
        pick_kernel,
        out_shape=jax.ShapeDtypeStruct((DEVICES, ROWS, BLK), jnp.int16),
        in_specs=[smem, smem, vmem, vmem, vmem],
        out_specs=vmem,
        scratch_shapes=[pltpu.VMEM((BUCKETS, ROWS, BLK), jnp.int16)],
        compiler_params=pltpu.CompilerParams(vmem_limit_bytes=VMEM_SMALL),
    )(flags, index, own, other, mirror)


def pack(value):
    most = jnp.max(jnp.abs(value), axis=0, keepdims=True)
    power = jnp.ceil(jnp.log2(jnp.maximum(most, TINY)))
    scaled = jnp.floor(value * jnp.exp2(BITS - power) + 0.5).astype(jnp.int32)
    rows, _ = row_col(value.shape)
    return jnp.where(rows > BLK, power.astype(jnp.int32), scaled).astype(jnp.int16)


def unpack(coded):
    wide = coded.astype(jnp.int32).astype(jnp.float32)
    return wide * jnp.exp2(wide[BLK + 1 : BLK + 2] - BITS)


def batch_kernel(
    count,
    blocks_in,
    basis_in,
    coarse,
    turned_in,
    core,
    weights,
    density,
    pieces,
    blocks,
    basis,
    turned,
    high,
    fine,
    total,
    scaled,
    arrived,
):
    def chunk(k, source, target, at):
        lanes = (slice(None), slice(k * CHUNK, (k + 1) * CHUNK))
        return pltpu.make_async_copy(source.at[lanes], target.at[lanes], arrived.at[at])

    chunks = [chunk(k, basis_in, basis, k) for k in range(COLS // CHUNK)]
    load_blocks = pltpu.make_async_copy(blocks_in, blocks, arrived.at[len(chunks)])
    load_turned = pltpu.make_async_copy(turned_in, turned, arrived.at[len(chunks) + 1])
    load_blocks.start()
    chunks[0].start()

    rows, cols = row_col((BLK, BLK))

    def message(device):
        return blocks[device].astype(jnp.int32).astype(jnp.float32)

    def place(side, start, right, value):
        top = value.astype(jnp.bfloat16)
        at = pl.ds(start, BLK)
        high[side, at, right * BLK : (right + 1) * BLK] = top
        rest = (value - top.astype(jnp.float32)).astype(jnp.float8_e4m3fn)
        fine[side, at, right * BLK : (right + 1) * BLK] = rest

    def place_pair(big, p):
        for di in range(2):
            for dj in range(2):
                device = (2 * p + di) * INNERS + big if di == dj else (2 * big + dj) * INNERS + p
                start = p * PAIR + di * BLK
                place(big % 2, start, dj, message(device)[:BLK])

    def place_diagonal(big):
        first = message(2 * big * INNERS + big)
        second = message((2 * big + 1) * INNERS + big)
        diagonal = jnp.broadcast_to(first[BLK : BLK + 1], (BLK, BLK))
        first, second = first[:BLK], second[:BLK]
        cross = jnp.where(rows > cols, first, jnp.where(rows < cols, second, diagonal))
        side, start = big % 2, big * PAIR
        place(side, start, 0, jnp.where(rows <= cols, first, 0.0))
        place(side, start, 1, cross)
        place(side, start + BLK, 0, jnp.zeros((BLK, BLK), jnp.float32))
        place(side, start + BLK, 1, jnp.where(rows >= cols, second, 0.0))

    load_blocks.wait()
    place_diagonal(0)
    tiles = PTS // TILE
    for big in range(KB // 2):
        depth = (big + 1) * PAIR
        if big * PAIR % CHUNK == 0:
            k = big * PAIR // CHUNK
            chunks[k].wait()
            if k + 1 < len(chunks):
                chunks[k + 1].start()
            else:
                load_turned.start()

        for m in range(tiles):
            if big + 1 < KB // 2:
                for p in range(m, big + 1, tiles):
                    place_pair(big + 1, p)
            at = slice(m * TILE, (m + 1) * TILE)
            side = big % 2
            product = jnp.dot(basis[at, :depth], high[side, :depth], preferred_element_type=jnp.float32)
            product += jnp.dot(coarse[at, :depth], fine[side, :depth], preferred_element_type=jnp.float32)
            product *= basis[at, big * PAIR : (big + 1) * PAIR].astype(jnp.float32)
            folded = product[:, :BLK] + product[:, BLK:]
            total[at] = folded if big == 0 else total[at] + folded
        if big + 1 < KB // 2:
            place_diagonal(big + 1)

    lines = [slice(k * BLK, (k + 1) * BLK) for k in range(LINES)]
    summed = jnp.concatenate([jnp.sum(total[at].T, axis=0, keepdims=True) for at in lines], axis=0)
    found = core[...] + summed * (1.0 / STEP)
    density[...] = found
    potential = slater_factor * jnp.exp(jnp.log(jnp.maximum(found, density_floor)) * (1.0 / 3.0))
    line, lane = row_col((LINES, BLK))
    integrand = jnp.where(line * BLK + lane < count[0], weights[...] * potential, 0.0)
    for k, at in enumerate(lines):
        total[at] = jnp.broadcast_to(integrand[k : k + 1], (BLK, BLK)).T

    tail = jnp.zeros((ROWS - BLK, BLK), jnp.float32)

    def send(device, value, last=tail):
        pieces[device] = pack(jnp.concatenate([value, last], axis=0))

    def weigh(big, low, high_end):
        for k in range(2):
            lanes = slice(big * PAIR + k * BLK, big * PAIR + (k + 1) * BLK)
            at = slice(low, high_end)
            part_of = (total[at] * basis[at, lanes].astype(jnp.float32)).astype(jnp.bfloat16)
            scaled[big % 2, at, k * BLK : (k + 1) * BLK] = part_of

    weigh(0, 0, PTS)
    load_turned.wait()
    for big in range(KB // 2):
        cuts = [PTS // 16 * k // (big + 1) * 16 for k in range(big + 2)]
        for part in range(big + 1):
            product = jnp.dot(
                turned[part * PAIR : (part + 1) * PAIR], scaled[big % 2], preferred_element_type=jnp.float32
            )
            if big + 1 < KB // 2:
                weigh(big + 1, cuts[part], cuts[part + 1])
            i, j = 2 * part, 2 * big
            if part < big:
                for di in range(2):
                    for dj in range(2):
                        send(
                            owner(i + di, j + dj),
                            product[di * BLK : (di + 1) * BLK, dj * BLK : (dj + 1) * BLK],
                        )
            else:
                cross = product[:BLK, BLK:]
                diagonal = jnp.sum(jnp.where(rows == cols, cross, 0.0), axis=0, keepdims=True)
                last = jnp.broadcast_to(diagonal, (ROWS - BLK, BLK))
                send(i * INNERS + big, jnp.where(rows > cols, cross, product[:BLK, :BLK]), last)
                send((i + 1) * INNERS + big, jnp.where(rows < cols, cross, product[BLK:, BLK:]), last)


def batch(count, blocks, basis, coarse, turned, core, weights):
    vmem = pl.BlockSpec(memory_space=pltpu.VMEM)
    anywhere = pl.BlockSpec(memory_space=pl.ANY)
    messages = (DEVICES, ROWS, BLK)
    return pl.pallas_call(
        batch_kernel,
        out_shape=(
            jax.ShapeDtypeStruct((LINES, BLK), jnp.float32),
            jax.ShapeDtypeStruct(messages, jnp.int16),
        ),
        in_specs=[pl.BlockSpec(memory_space=pltpu.SMEM)] + [anywhere, anywhere, vmem, anywhere, vmem, vmem],
        out_specs=(vmem, vmem),
        scratch_shapes=[
            pltpu.VMEM(messages, jnp.int16),
            pltpu.VMEM((PTS, COLS), jnp.bfloat16),
            pltpu.VMEM((COLS, PTS), jnp.bfloat16),
            pltpu.VMEM((2, COLS, PAIR), jnp.bfloat16),
            pltpu.VMEM((2, COLS, PAIR), jnp.float8_e4m3fn),
            pltpu.VMEM((PTS, BLK), jnp.float32),
            pltpu.VMEM((2, PTS, PAIR), jnp.bfloat16),
            pltpu.SemaphoreType.DMA((COLS // CHUNK + 2,)),
        ],
        compiler_params=pltpu.CompilerParams(vmem_limit_bytes=VMEM_BATCH),
    )(count, blocks, basis, coarse, turned, core, weights)


def sum_kernel(index, pieces, total, copy):
    total[...] = jnp.zeros_like(total)

    def add(k, carry):
        at = index[k]
        total[at] = total[at] + unpack(pieces[k])
        return carry

    lax.fori_loop(0, DEVICES, add, 0, unroll=4)
    for k in range(BUCKETS):
        copy[k] = pack(total[k])


def sum_pieces(index, pieces):
    shape = (BUCKETS, ROWS, BLK)
    vmem = pl.BlockSpec(memory_space=pltpu.VMEM)
    return pl.pallas_call(
        sum_kernel,
        out_shape=(jax.ShapeDtypeStruct(shape, jnp.float32), jax.ShapeDtypeStruct(shape, jnp.int16)),
        in_specs=[pl.BlockSpec(memory_space=pltpu.SMEM), vmem],
        out_specs=(vmem, vmem),
        compiler_params=pltpu.CompilerParams(vmem_limit_bytes=VMEM_SMALL),
    )(index, pieces)


def finish_kernel(flags, total, mirror, out):
    flip = flags[0] == 1
    special = flags[1] == 1
    half = flags[3]
    rows, cols = row_col((BLK, BLK))

    def slot(which, a, b):
        start = pl.multiple_of(which * SLOT + b * BLK, BLK)
        return (slice(a * BLK, (a + 1) * BLK), pl.ds(start, BLK))

    def received(k):
        return unpack(mirror[k])

    @pl.when(jnp.logical_not(special))
    def _():
        for a in range(SPAN):
            for b in range(SPAN):
                k = a * SPAN + b

                @pl.when(flip)
                def _():
                    out[slot(half, b, a)] = total[k, :BLK].T
                    out[slot(1 - half, b, a)] = received(k)[:BLK].T

                @pl.when(jnp.logical_not(flip))
                def _():
                    out[slot(half, a, b)] = total[k, :BLK]
                    out[slot(1 - half, a, b)] = received(k)[:BLK]

    def diagonal_group(lower):
        for a in range(SPAN):
            for b in range(SPAN):
                k = a * SPAN + b
                mine, theirs = total[k], received(k)
                first, second = (mine, theirs) if lower else (theirs, mine)
                middle = jnp.broadcast_to(first[BLK : BLK + 1], (BLK, BLK))
                cross = jnp.where(
                    rows > cols, first[:BLK], jnp.where(rows < cols, second[:BLK], middle)
                )
                if lower:
                    out[slot(half, a, b)] = cross
                else:
                    out[slot(half, b, a)] = cross.T
                if a != b:
                    out[slot(1 - half, a, b)] = jnp.zeros((BLK, BLK), jnp.float32)
        for a in range(SPAN):
            held = jnp.zeros((BLK, BLK), jnp.float32)
            for b in range(SPAN):
                held += total[a * SPAN + b if lower else b * SPAN + a, :BLK]
            keep = rows < cols if lower else rows > cols
            strict = jnp.where(keep, held, 0.0)
            out[slot(1 - half, a, a)] = jnp.where(rows == cols, held, strict + strict.T)

    @pl.when(jnp.logical_and(special, flags[2] == 1))
    def _():
        diagonal_group(True)

    @pl.when(jnp.logical_and(special, flags[2] == 0))
    def _():
        diagonal_group(False)


def finish(flags, total, mirror):
    vmem = pl.BlockSpec(memory_space=pltpu.VMEM)
    return pl.pallas_call(
        finish_kernel,
        out_shape=jax.ShapeDtypeStruct((SLOT, 2 * SLOT), jnp.float32),
        in_specs=[pl.BlockSpec(memory_space=pltpu.SMEM), vmem, vmem],
        out_specs=vmem,
        compiler_params=pltpu.CompilerParams(vmem_limit_bytes=VMEM_SMALL),
    )(flags, total, mirror)


def per_device(density_matrix, basis_values, block_list, point_counts, core_density, grid_weights):
    g = lax.axis_index("group")
    n = lax.axis_index("inner")
    odd = lax.rem(g, 2)
    half = jnp.where(g < 2 * n, odd, 1 - odd)
    flip = (g > 2 * n).astype(jnp.int32)
    special = g // 2 == n
    column_slot = 2 * n + half
    first, second = jnp.minimum(g, column_slot), jnp.maximum(g, column_slot)
    flags = jnp.stack([flip, special.astype(jnp.int32), 1 - odd, half]).astype(jnp.int32)
    pairs = mirror_pairs()

    basis = basis_values[0]
    left, right = density_matrix[:, :SLOT], density_matrix[:, SLOT:]
    own = jnp.where(half == 0, left, right)
    other = jnp.where(half == 0, right, left)
    sent = jnp.where(special, own, other)
    mirror = lax.ppermute(sent, AXES, pairs)
    lists = lax.all_to_all(
        jnp.broadcast_to(block_list, (DEVICES, KB)), AXES, split_axis=0, concat_axis=0, tiled=True
    )
    slots = jnp.arange(KB, dtype=jnp.int32)
    factor = jnp.where(slots == first, SPAN, 0) + jnp.where(slots == second, 1, 0)
    index = jnp.sum((lists - slots * SPAN) * factor, axis=1).astype(jnp.int32)

    picked = pick(flags, index, own, other, mirror)
    blocks = lax.all_to_all(picked, AXES, split_axis=0, concat_axis=0, tiled=True)
    density, pieces = batch(
        point_counts,
        blocks,
        basis,
        basis.astype(jnp.float8_e4m3fn),
        basis.T,
        core_density.reshape(LINES, BLK),
        grid_weights.reshape(LINES, BLK),
    )
    landed = lax.all_to_all(pieces, AXES, split_axis=0, concat_axis=0, tiled=True)
    total, copy = sum_pieces(index, landed)
    returned = lax.ppermute(copy, AXES, [(target, source) for source, target in pairs])
    return density.reshape(1, PTS), finish(flags, total, returned)


def solution(mesh):
    return jax.shard_map(
        per_device,
        mesh=mesh,
        in_specs=(
            P("group", "inner"),
            P(AXES, None, None),
            P(AXES, None),
            P(AXES),
            P(AXES, None),
            P(AXES, None),
        ),
        out_specs=(P(AXES, None), P("group", "inner")),
        check_vma=False,
    )
```

```python
import jax
import jax.numpy as jnp
from jax import lax
from jax.experimental import pallas as pl
from jax.experimental.pallas import tpu as pltpu
from jax.sharding import PartitionSpec as P

BLK = 128
KB = 16
GROUPS = 16
INNERS = 8
DEVICES = GROUPS * INNERS
SPAN = 4
SLOT = SPAN * BLK
BUCKETS = SPAN * SPAN
ROWS = BLK + 8
PTS = 1536
LINES = PTS // BLK
COLS = KB * BLK
PAIR = 2 * BLK
AXES = ("group", "inner")

slater_factor = -((3.0 / 3.141592653589793) ** (1.0 / 3.0))
density_floor = 0.1
STEP = float(2**22)
BITS = 14.0
TINY = 2.0**-100
TILE = 256
CHUNK = 512
VMEM_BATCH = 38 * 2**20
VMEM_SMALL = 24 * 2**20


def owner(i, j):
    return i * INNERS + j // 2 if (i + j) % 2 == 0 else j * INNERS + i // 2


def chosen_half(g, n):
    odd = g % 2
    return odd if g < 2 * n else 1 - odd


def mirror_pairs():
    pairs = []
    for g in range(GROUPS):
        for n in range(INNERS):
            half = chosen_half(g, n)
            if g // 2 != n:
                half = 1 - half
            pairs.append((g * INNERS + n, (2 * n + half) * INNERS + g // 2))
    return pairs


def row_col(shape):
    return lax.broadcasted_iota(jnp.int32, shape, 0), lax.broadcasted_iota(jnp.int32, shape, 1)


def encode(value):
    return jnp.floor(value * STEP + 0.5).astype(jnp.int32).astype(jnp.int16)


def pick_kernel(flags, index, own, other, mirror, out, table):
    flip = flags[0] == 1
    special = flags[1] == 1
    low = flags[2] == 1

    def put(a, b, first, second):
        rows, cols = row_col((BLK, BLK))
        total = first + second.T

        @pl.when(jnp.logical_not(special))
        def _():
            tail = jnp.zeros((ROWS - BLK, BLK), jnp.float32)
            table[a * SPAN + b] = encode(jnp.concatenate([total, tail], axis=0))

        @pl.when(special)
        def _():
            diagonal = jnp.sum(jnp.where(rows == cols, total, 0.0), axis=0, keepdims=True)
            tail = jnp.broadcast_to(diagonal, (ROWS - BLK, BLK))
            at = jnp.where(low, a, b)
            start = pl.multiple_of(at * BLK, BLK)
            block = other[pl.ds(start, BLK), pl.ds(start, BLK)].astype(jnp.float32)
            both = jnp.where(rows == cols, block, block + block.T)
            keep = jnp.where(low, rows - cols, cols - rows) > 0
            packed = jnp.where(keep, total, both)
            table[a * SPAN + b] = encode(jnp.concatenate([packed, tail], axis=0))

    def block_of(ref, a, b):
        return ref[a * BLK : (a + 1) * BLK, b * BLK : (b + 1) * BLK].astype(jnp.float32)

    for a in range(SPAN):
        for b in range(SPAN):

            @pl.when(flip)
            def _():
                put(a, b, block_of(mirror, a, b), block_of(own, b, a))

            @pl.when(jnp.logical_not(flip))
            def _():
                put(a, b, block_of(own, a, b), block_of(mirror, b, a))

    def copy(k, carry):
        out[k] = table[index[k]]
        return carry

    lax.fori_loop(0, DEVICES, copy, 0, unroll=8)


def pick(flags, index, own, other, mirror):
    vmem = pl.BlockSpec(memory_space=pltpu.VMEM)
    smem = pl.BlockSpec(memory_space=pltpu.SMEM)
    return pl.pallas_call(
        pick_kernel,
        out_shape=jax.ShapeDtypeStruct((DEVICES, ROWS, BLK), jnp.int16),
        in_specs=[smem, smem, vmem, vmem, vmem],
        out_specs=vmem,
        scratch_shapes=[pltpu.VMEM((BUCKETS, ROWS, BLK), jnp.int16)],
        compiler_params=pltpu.CompilerParams(vmem_limit_bytes=VMEM_SMALL),
    )(flags, index, own, other, mirror)


def pack(value):
    most = jnp.max(jnp.abs(value), axis=0, keepdims=True)
    power = jnp.ceil(jnp.log2(jnp.maximum(most, TINY)))
    scaled = jnp.floor(value * jnp.exp2(BITS - power) + 0.5).astype(jnp.int32)
    rows, _ = row_col(value.shape)
    return jnp.where(rows > BLK, power.astype(jnp.int32), scaled).astype(jnp.int16)


def unpack(coded):
    wide = coded.astype(jnp.int32).astype(jnp.float32)
    return wide * jnp.exp2(wide[BLK + 1 : BLK + 2] - BITS)


def batch_kernel(
    count,
    blocks_in,
    basis_in,
    coarse,
    turned_in,
    core,
    weights,
    density,
    pieces,
    blocks,
    basis,
    turned,
    high,
    fine,
    total,
    scaled,
    arrived,
):
    def chunk(k, source, target, at):
        lanes = (slice(None), slice(k * CHUNK, (k + 1) * CHUNK))
        return pltpu.make_async_copy(source.at[lanes], target.at[lanes], arrived.at[at])

    chunks = [chunk(k, basis_in, basis, k) for k in range(COLS // CHUNK)]
    load_blocks = pltpu.make_async_copy(blocks_in, blocks, arrived.at[len(chunks)])
    load_turned = pltpu.make_async_copy(turned_in, turned, arrived.at[len(chunks) + 1])
    load_blocks.start()
    chunks[0].start()

    rows, cols = row_col((BLK, BLK))

    def message(device):
        return blocks[device].astype(jnp.int32).astype(jnp.float32)

    def place(side, start, right, value):
        top = value.astype(jnp.bfloat16)
        at = pl.ds(start, BLK)
        high[side, at, right * BLK : (right + 1) * BLK] = top
        rest = (value - top.astype(jnp.float32)).astype(jnp.float8_e4m3fn)
        fine[side, at, right * BLK : (right + 1) * BLK] = rest

    def place_pair(big, p):
        for di in range(2):
            for dj in range(2):
                device = (2 * p + di) * INNERS + big if di == dj else (2 * big + dj) * INNERS + p
                start = p * PAIR + di * BLK
                place(big % 2, start, dj, message(device)[:BLK])

    def place_diagonal(big):
        first = message(2 * big * INNERS + big)
        second = message((2 * big + 1) * INNERS + big)
        diagonal = jnp.broadcast_to(first[BLK : BLK + 1], (BLK, BLK))
        first, second = first[:BLK], second[:BLK]
        cross = jnp.where(rows > cols, first, jnp.where(rows < cols, second, diagonal))
        side, start = big % 2, big * PAIR
        place(side, start, 0, jnp.where(rows <= cols, first, 0.0))
        place(side, start, 1, cross)
        place(side, start + BLK, 0, jnp.zeros((BLK, BLK), jnp.float32))
        place(side, start + BLK, 1, jnp.where(rows >= cols, second, 0.0))

    load_blocks.wait()
    place_diagonal(0)
    tiles = PTS // TILE
    for big in range(KB // 2):
        depth = (big + 1) * PAIR
        if big * PAIR % CHUNK == 0:
            k = big * PAIR // CHUNK
            chunks[k].wait()
            if k + 1 < len(chunks):
                chunks[k + 1].start()
            else:
                load_turned.start()

        for m in range(tiles):
            if big + 1 < KB // 2:
                for p in range(m, big + 1, tiles):
                    place_pair(big + 1, p)
            at = slice(m * TILE, (m + 1) * TILE)
            side = big % 2
            product = jnp.dot(basis[at, :depth], high[side, :depth], preferred_element_type=jnp.float32)
            product += jnp.dot(coarse[at, :depth], fine[side, :depth], preferred_element_type=jnp.float32)
            product *= basis[at, big * PAIR : (big + 1) * PAIR].astype(jnp.float32)
            folded = product[:, :BLK] + product[:, BLK:]
            total[at] = folded if big == 0 else total[at] + folded
        if big + 1 < KB // 2:
            place_diagonal(big + 1)

    lines = [slice(k * BLK, (k + 1) * BLK) for k in range(LINES)]
    summed = jnp.concatenate([jnp.sum(total[at].T, axis=0, keepdims=True) for at in lines], axis=0)
    found = core[...] + summed * (1.0 / STEP)
    density[...] = found
    potential = slater_factor * jnp.exp(jnp.log(jnp.maximum(found, density_floor)) * (1.0 / 3.0))
    line, lane = row_col((LINES, BLK))
    integrand = jnp.where(line * BLK + lane < count[0], weights[...] * potential, 0.0)
    for k, at in enumerate(lines):
        total[at] = jnp.broadcast_to(integrand[k : k + 1], (BLK, BLK)).T

    tail = jnp.zeros((ROWS - BLK, BLK), jnp.float32)

    def send(device, value, last=tail):
        pieces[device] = pack(jnp.concatenate([value, last], axis=0))

    def weigh(big, low, high_end):
        for k in range(2):
            lanes = slice(big * PAIR + k * BLK, big * PAIR + (k + 1) * BLK)
            at = slice(low, high_end)
            part_of = (total[at] * basis[at, lanes].astype(jnp.float32)).astype(jnp.bfloat16)
            scaled[big % 2, at, k * BLK : (k + 1) * BLK] = part_of

    weigh(0, 0, PTS)
    load_turned.wait()
    for big in range(KB // 2):
        cuts = [PTS // 16 * k // (big + 1) * 16 for k in range(big + 2)]
        for part in range(big + 1):
            product = jnp.dot(
                turned[part * PAIR : (part + 1) * PAIR], scaled[big % 2], preferred_element_type=jnp.float32
            )
            if big + 1 < KB // 2:
                weigh(big + 1, cuts[part], cuts[part + 1])
            i, j = 2 * part, 2 * big
            if part < big:
                for di in range(2):
                    for dj in range(2):
                        send(
                            owner(i + di, j + dj),
                            product[di * BLK : (di + 1) * BLK, dj * BLK : (dj + 1) * BLK],
                        )
            else:
                cross = product[:BLK, BLK:]
                diagonal = jnp.sum(jnp.where(rows == cols, cross, 0.0), axis=0, keepdims=True)
                last = jnp.broadcast_to(diagonal, (ROWS - BLK, BLK))
                send(i * INNERS + big, jnp.where(rows > cols, cross, product[:BLK, :BLK]), last)
                send((i + 1) * INNERS + big, jnp.where(rows < cols, cross, product[BLK:, BLK:]), last)


def batch(count, blocks, basis, coarse, turned, core, weights):
    vmem = pl.BlockSpec(memory_space=pltpu.VMEM)
    anywhere = pl.BlockSpec(memory_space=pl.ANY)
    messages = (DEVICES, ROWS, BLK)
    return pl.pallas_call(
        batch_kernel,
        out_shape=(
            jax.ShapeDtypeStruct((LINES, BLK), jnp.float32),
            jax.ShapeDtypeStruct(messages, jnp.int16),
        ),
        in_specs=[pl.BlockSpec(memory_space=pltpu.SMEM)] + [anywhere, anywhere, vmem, anywhere, vmem, vmem],
        out_specs=(vmem, vmem),
        scratch_shapes=[
            pltpu.VMEM(messages, jnp.int16),
            pltpu.VMEM((PTS, COLS), jnp.bfloat16),
            pltpu.VMEM((COLS, PTS), jnp.bfloat16),
            pltpu.VMEM((2, COLS, PAIR), jnp.bfloat16),
            pltpu.VMEM((2, COLS, PAIR), jnp.float8_e4m3fn),
            pltpu.VMEM((PTS, BLK), jnp.float32),
            pltpu.VMEM((2, PTS, PAIR), jnp.bfloat16),
            pltpu.SemaphoreType.DMA((COLS // CHUNK + 2,)),
        ],
        compiler_params=pltpu.CompilerParams(vmem_limit_bytes=VMEM_BATCH),
    )(count, blocks, basis, coarse, turned, core, weights)


def sum_kernel(index, pieces, total, copy):
    total[...] = jnp.zeros_like(total)

    def add(k, carry):
        at = index[k]
        total[at] = total[at] + unpack(pieces[k])
        return carry

    lax.fori_loop(0, DEVICES, add, 0, unroll=8)
    for k in range(BUCKETS):
        copy[k] = pack(total[k])


def sum_pieces(index, pieces):
    shape = (BUCKETS, ROWS, BLK)
    vmem = pl.BlockSpec(memory_space=pltpu.VMEM)
    return pl.pallas_call(
        sum_kernel,
        out_shape=(jax.ShapeDtypeStruct(shape, jnp.float32), jax.ShapeDtypeStruct(shape, jnp.int16)),
        in_specs=[pl.BlockSpec(memory_space=pltpu.SMEM), vmem],
        out_specs=(vmem, vmem),
        compiler_params=pltpu.CompilerParams(vmem_limit_bytes=VMEM_SMALL),
    )(index, pieces)


def half_of(ref, which):
    return ref.at[:, pl.ds(pl.multiple_of(which * SLOT, SLOT), SLOT)]


def lay_out(flip, held, block_of):
    for a in range(SPAN):
        for b in range(SPAN):
            k = a * SPAN + b

            @pl.when(flip)
            def _():
                held[b * BLK : (b + 1) * BLK, a * BLK : (a + 1) * BLK] = block_of(k).T

            @pl.when(jnp.logical_not(flip))
            def _():
                held[a * BLK : (a + 1) * BLK, b * BLK : (b + 1) * BLK] = block_of(k)


def own_kernel(flags, total, out, held, done):
    @pl.when(flags[1] == 0)
    def _():
        lay_out(flags[0] == 1, held, lambda k: total[k, :BLK])
        copy = pltpu.make_async_copy(held, half_of(out, flags[3]), done)
        copy.start()
        copy.wait()


def finish_own(flags, total):
    vmem = pl.BlockSpec(memory_space=pltpu.VMEM)
    return pl.pallas_call(
        own_kernel,
        out_shape=jax.ShapeDtypeStruct((SLOT, 2 * SLOT), jnp.float32),
        in_specs=[pl.BlockSpec(memory_space=pltpu.SMEM), vmem],
        out_specs=pl.BlockSpec(memory_space=pl.ANY),
        scratch_shapes=[pltpu.VMEM((SLOT, SLOT), jnp.float32), pltpu.SemaphoreType.DMA],
        compiler_params=pltpu.CompilerParams(vmem_limit_bytes=VMEM_SMALL),
    )(flags, total)


def finish_kernel(flags, total, mirror, partly, out, held, whole, done):
    flip = flags[0] == 1
    special = flags[1] == 1
    half = flags[3]
    rows, cols = row_col((BLK, BLK))

    def slot(which, a, b):
        start = pl.multiple_of(which * SLOT + b * BLK, BLK)
        return (slice(a * BLK, (a + 1) * BLK), pl.ds(start, BLK))

    def received(k):
        return unpack(mirror[k])

    @pl.when(jnp.logical_not(special))
    def _():
        lay_out(flip, held, lambda k: received(k)[:BLK])
        copy = pltpu.make_async_copy(held, half_of(out, 1 - half), done)
        copy.start()
        copy.wait()

    def diagonal_group(lower):
        for a in range(SPAN):
            for b in range(SPAN):
                k = a * SPAN + b
                mine, theirs = total[k], received(k)
                first, second = (mine, theirs) if lower else (theirs, mine)
                middle = jnp.broadcast_to(first[BLK : BLK + 1], (BLK, BLK))
                cross = jnp.where(
                    rows > cols, first[:BLK], jnp.where(rows < cols, second[:BLK], middle)
                )
                if lower:
                    whole[slot(half, a, b)] = cross
                else:
                    whole[slot(half, b, a)] = cross.T
                if a != b:
                    whole[slot(1 - half, a, b)] = jnp.zeros((BLK, BLK), jnp.float32)
        for a in range(SPAN):
            held = jnp.zeros((BLK, BLK), jnp.float32)
            for b in range(SPAN):
                held += total[a * SPAN + b if lower else b * SPAN + a, :BLK]
            keep = rows < cols if lower else rows > cols
            strict = jnp.where(keep, held, 0.0)
            whole[slot(1 - half, a, a)] = jnp.where(rows == cols, held, strict + strict.T)

    @pl.when(special)
    def _():
        @pl.when(flags[2] == 1)
        def _():
            diagonal_group(True)

        @pl.when(flags[2] == 0)
        def _():
            diagonal_group(False)

        copy = pltpu.make_async_copy(whole, out, done)
        copy.start()
        copy.wait()


def finish(flags, total, mirror, partly):
    vmem = pl.BlockSpec(memory_space=pltpu.VMEM)
    anywhere = pl.BlockSpec(memory_space=pl.ANY)
    return pl.pallas_call(
        finish_kernel,
        out_shape=jax.ShapeDtypeStruct((SLOT, 2 * SLOT), jnp.float32),
        in_specs=[pl.BlockSpec(memory_space=pltpu.SMEM), vmem, vmem, anywhere],
        out_specs=anywhere,
        scratch_shapes=[
            pltpu.VMEM((SLOT, SLOT), jnp.float32),
            pltpu.VMEM((SLOT, 2 * SLOT), jnp.float32),
            pltpu.SemaphoreType.DMA,
        ],
        input_output_aliases={3: 0},
        compiler_params=pltpu.CompilerParams(vmem_limit_bytes=VMEM_SMALL),
    )(flags, total, mirror, partly)


def per_device(density_matrix, basis_values, block_list, point_counts, core_density, grid_weights):
    g = lax.axis_index("group")
    n = lax.axis_index("inner")
    odd = lax.rem(g, 2)
    half = jnp.where(g < 2 * n, odd, 1 - odd)
    flip = (g > 2 * n).astype(jnp.int32)
    special = g // 2 == n
    column_slot = 2 * n + half
    first, second = jnp.minimum(g, column_slot), jnp.maximum(g, column_slot)
    flags = jnp.stack([flip, special.astype(jnp.int32), 1 - odd, half]).astype(jnp.int32)
    pairs = mirror_pairs()

    basis = basis_values[0]
    left, right = density_matrix[:, :SLOT], density_matrix[:, SLOT:]
    own = jnp.where(half == 0, left, right)
    other = jnp.where(half == 0, right, left)
    sent = jnp.where(special, own, other)
    mirror = lax.ppermute(sent, AXES, pairs)
    lists = lax.all_to_all(
        jnp.broadcast_to(block_list, (DEVICES, KB)), AXES, split_axis=0, concat_axis=0, tiled=True
    )
    slots = jnp.arange(KB, dtype=jnp.int32)
    factor = jnp.where(slots == first, SPAN, 0) + jnp.where(slots == second, 1, 0)
    index = jnp.sum((lists - slots * SPAN) * factor, axis=1).astype(jnp.int32)

    picked = pick(flags, index, own, other, mirror)
    blocks = lax.all_to_all(picked, AXES, split_axis=0, concat_axis=0, tiled=True)
    density, pieces = batch(
        point_counts,
        blocks,
        basis,
        basis.astype(jnp.float8_e4m3fn),
        basis.T,
        core_density.reshape(LINES, BLK),
        grid_weights.reshape(LINES, BLK),
    )
    landed = lax.all_to_all(pieces, AXES, split_axis=0, concat_axis=0, tiled=True)
    total, copy = sum_pieces(index, landed)
    returned = lax.ppermute(copy, AXES, [(target, source) for source, target in pairs])
    partly = finish_own(flags, total)
    return density.reshape(1, PTS), finish(flags, total, returned, partly)


def solution(mesh):
    return jax.shard_map(
        per_device,
        mesh=mesh,
        in_specs=(
            P("group", "inner"),
            P(AXES, None, None),
            P(AXES, None),
            P(AXES),
            P(AXES, None),
            P(AXES, None),
        ),
        out_specs=(P(AXES, None), P("group", "inner")),
        check_vma=False,
    )
```
